128 devices in a mesh: ctx: 32 (over z, y, x_lo), tp: 4 (over x_hi, core).
Axes of the slice: x: 4 (x_hi: 2, x_lo: 2; x = x_hi * 2 + x_lo), y: 4, z: 4, core: 2. Of those that a mesh axis runs over, the one named last changes fastest.
Arguments:
- query_gate: bfloat16 [2048, 16384], P('tp', 'ctx'), may hold values from -6 to 6
- key_branch: bfloat16 [2048, 16384], P('tp', 'ctx'), may hold values from -6 to 6
- value_branch: bfloat16 [2048, 16384], P('tp', 'ctx'), may hold values from -6 to 6
- filter_taps: float32 [2048, 16384], P(('tp', 'ctx')), may hold values from -2 to 2
- skip_gain: float32 [2048], P(('tp', 'ctx')), may hold values from -4 to 4
- out_weight: bfloat16 [2048, 4096], P('tp'), may hold values from -0.09375 to 0.09375
- out_grad: bfloat16 [16384, 4096], P('ctx', 'tp'), may hold values from -6 to 6
Outputs:
- grad_query: bfloat16 [2048, 16384], P('tp', 'ctx')
- grad_key: bfloat16 [2048, 16384], P('tp', 'ctx')
- grad_value: bfloat16 [2048, 16384], P('tp', 'ctx')
- grad_filter: float32 [2048, 16384], P(('tp', 'ctx'))
- grad_skip: float32 [2048], P(('tp', 'ctx'))
- grad_weight: float32 [2048, 4096], P('tp', 'ctx')
The draws below stay inside these ranges and needn't reach their ends.
All inputs are finite; a program needn't handle non-finite values.
Results may differ from the reference program's by a relative error of at most 0.0058.
Values may be sent and summed in bfloat16 or wider, within the bound.
A program may use at most 128 MiB of HBM per device.

```python
import jax
import jax.numpy as jnp

D = 4096
CH = 2048
LEN = 16384


def draw_filter_taps(key, part):
    key = jax.random.fold_in(key, 7)
    key_pick, key_slow, key_fast, key_noise = jax.random.split(key, 4)
    slow_rate = jnp.exp(jax.random.uniform(key_slow, (CH, 1), jnp.float32, jnp.log(0.3 / LEN), jnp.log(2.0 / LEN)))
    fast_rate = jnp.exp(jax.random.uniform(key_fast, (CH, 1), jnp.float32, jnp.log(1.0 / 50.0), jnp.log(1.0 / 10.0)))
    picked = jax.random.uniform(key_pick, (CH, 1), jnp.float32) < 0.5
    rate = jnp.where(picked, slow_rate, fast_rate)
    lags = jnp.arange(LEN, dtype=jnp.float32)[None, :]
    envelope = jnp.exp(-rate * lags)
    scale = jnp.sqrt(-jnp.expm1(-2.0 * rate) / -jnp.expm1(-2.0 * rate * LEN))
    noise = jnp.clip(jax.random.normal(key_noise, (CH, LEN), jnp.float32), -4.0, 4.0)
    return noise * envelope * scale


def strengthened(array, stream_key, source, target, parts, factor):
    def block_of(axis_at):
        return (jnp.arange(array.shape[axis_at]) // (array.shape[axis_at] // parts)).reshape((-1,) + (1,) * (array.ndim - 1 - axis_at))

    first = jax.random.permutation(stream_key, parts)[block_of(target)]
    second = (block_of(target) + parts // 2) % parts
    return jnp.where((block_of(source) == first) | (block_of(source) == second), factor * array, array)


def block_levels(stream_key, shape, cuts, smallest, largest):
    factor_of = 1.0
    for position, shards_of in cuts:
        heights = jax.random.uniform(jax.random.fold_in(jax.random.fold_in(stream_key, 6), position), (shards_of,), jnp.float32, smallest / len(cuts), largest / len(cuts))
        factor_of = factor_of * jnp.repeat(jnp.exp(heights), shape[position] // shards_of).reshape((-1,) + (1,) * (len(shape) - 1 - position))
    return factor_of


def centred(own_key, dims, scale, bound, pieces=(), held_as=jnp.bfloat16):
    values = scale * jax.random.normal(own_key, dims, jnp.float32)
    if pieces:
        values = values * block_levels(own_key, dims, pieces, -0.22, 0.18)
    return jnp.clip(values, -bound, bound).astype(held_as)


def bell_draw_with(rng, dims, deviation, reach, cuts, heavy, kind=jnp.bfloat16):
    values = deviation * jax.random.normal(rng, dims, jnp.float32)
    if cuts:
        values = values * block_levels(rng, dims, cuts, -0.22, 0.18)
    return jnp.clip(strengthened(values, jax.random.fold_in(rng, 3), *heavy), -reach, reach).astype(kind)


def setup_inputs(seed: int = 0) -> dict:
    key_list = jax.random.split(jax.random.key(seed), 8)
    return {
        "query_gate": centred(key_list[0], (CH, LEN), 1.0, 6.0, ((0, 4), (1, 32))),
        "key_branch": centred(key_list[1], (CH, LEN), 1.0, 6.0, ((0, 4), (1, 32))),
        "value_branch": centred(key_list[2], (CH, LEN), 1.0, 6.0, ((0, 4), (1, 32))),
        "filter_taps": draw_filter_taps(jax.random.fold_in(key_list[7], 71), 0),
        "skip_gain": centred(key_list[4], (CH,), 1.0, 4.0, ((0, 128),), jnp.float32),
        "out_weight": centred(key_list[5], (CH, D), D ** -0.5, 0.09375, ((0, 4),)),
        "out_grad": bell_draw_with(key_list[6], (LEN, D), 1.0, 6.0, ((0, 32), (1, 4)), (0, 1, 32, 2.75)),
    }


def reference(query_gate, key_branch, value_branch, filter_taps, skip_gain, out_weight, out_grad):
    size = 2 * LEN
    gated = (key_branch.astype(jnp.float32) * value_branch.astype(jnp.float32)).astype(jnp.bfloat16)
    gated_f = gated.astype(jnp.float32)
    filter_spec = jnp.fft.fft(filter_taps, n=size, axis=1)
    gated_spec = jnp.fft.fft(gated_f, n=size, axis=1)
    conv_full = jnp.real(jnp.fft.ifft(filter_spec * gated_spec, axis=1))[:, :LEN]
    conv_out = (conv_full + skip_gain[:, None] * gated_f).astype(jnp.bfloat16)
    conv_f = conv_out.astype(jnp.float32)
    query_f = query_gate.astype(jnp.float32)
    mixed = (query_f * conv_f).astype(jnp.bfloat16)
    grad_mixed = jnp.dot(out_weight, out_grad.T, preferred_element_type=jnp.float32)
    grad_conv = (grad_mixed * query_f).astype(jnp.bfloat16)
    grad_conv_f = grad_conv.astype(jnp.float32)
    grad_spec = jnp.fft.fft(grad_conv_f, n=size, axis=1)
    back_full = jnp.real(jnp.fft.ifft(jnp.conj(filter_spec) * grad_spec, axis=1))[:, :LEN]
    grad_gated = (back_full + skip_gain[:, None] * grad_conv_f).astype(jnp.bfloat16)
    grad_filter = jnp.real(jnp.fft.ifft(grad_spec * jnp.conj(gated_spec), axis=1))[:, :LEN].astype(jnp.float32)
    grad_skip = jnp.sum(grad_conv_f * gated_f, axis=1)
    grad_query = (grad_mixed * conv_f).astype(jnp.bfloat16)
    grad_gated_f = grad_gated.astype(jnp.float32)
    grad_key = (grad_gated_f * value_branch.astype(jnp.float32)).astype(jnp.bfloat16)
    grad_value = (grad_gated_f * key_branch.astype(jnp.float32)).astype(jnp.bfloat16)
    grad_weight = jnp.dot(mixed, out_grad, preferred_element_type=jnp.float32)
    return grad_query, grad_key, grad_value, grad_filter, grad_skip, grad_weight
```

```python
import numpy as np
import ml_dtypes
import jax
import jax.numpy as jnp
from jax import lax
from jax.experimental import pallas as pl
from jax.experimental.pallas import tpu as pltpu
from jax.sharding import PartitionSpec as P

ROWS = 64
COLS = 256
LANES = 128
CHANS = 16
SEQ_BLOCKS = 32


def bf16_pair(values):
    high = values.astype(ml_dtypes.bfloat16)
    low = (values - high.astype(np.float64)).astype(ml_dtypes.bfloat16)
    return high, low


def tables():
    ka = np.arange(ROWS) + 0.5
    phase_a = 2.0 * np.pi * np.outer(ka, np.arange(ROWS)) / (2 * ROWS)
    first = np.concatenate([np.cos(phase_a), -np.sin(phase_a)], axis=0)
    high, low = bf16_pair(first)
    first = np.concatenate([high, low, high], axis=1)
    last = np.concatenate([np.cos(phase_a).T, np.sin(phase_a).T], axis=1) / (ROWS * COLS)
    last = last.astype(ml_dtypes.bfloat16)
    last = np.concatenate([last, last], axis=1)
    phase_t = 2.0 * np.pi * np.outer(ka, np.arange(COLS)) / (2 * ROWS * COLS)
    turn = np.concatenate([np.cos(phase_t), np.sin(phase_t)], axis=1).astype(np.float32)
    phase_b = 2.0 * np.pi * (np.outer(np.arange(COLS), np.arange(COLS)) % COLS) / COLS
    cos_b, sin_b = np.cos(phase_b), np.sin(phase_b)
    second = np.block([[cos_b, -sin_b], [sin_b, cos_b]]).astype(ml_dtypes.bfloat16)
    return first, last, turn, second


def dot(left, right):
    return jnp.dot(left, right, preferred_element_type=jnp.float32)


def turned(re, im, turn_ref):
    cos, sin = turn_ref[:, :COLS], turn_ref[:, COLS:]
    return re * cos + im * sin, im * cos - re * sin


def take_blocks(blocks_ref, grid):
    def step(s, carry):
        block = blocks_ref[s].astype(jnp.float32)
        for part in range(4):
            rows = pl.ds(pl.multiple_of(s * 32 + part // 2 * CHANS, CHANS), CHANS)
            grid[part % 2, rows, :] = block[:, part * LANES : (part + 1) * LANES]
        return carry

    lax.fori_loop(0, SEQ_BLOCKS, step, 0, unroll=4)


def second_stage(mixed, second_ref, out):
    def step(i, carry):
        rows = pl.ds(pl.multiple_of(i * 256, 256), 256)
        out[rows, :] = dot(mixed[rows, :], second_ref[...])
        return carry

    lax.fori_loop(0, CHANS * ROWS // 256, step, 0)


def spectrum_of(grid, first_ref, turn_ref, second_ref, mixed, out, wide):
    def step(c, carry):
        rows = pl.ds(c, ROWS, stride=CHANS)
        signal = jnp.concatenate([grid[0, rows, :], grid[1, rows, :]], axis=1)
        high = signal.astype(jnp.bfloat16)
        if wide:
            low = (signal - high.astype(jnp.float32)).astype(jnp.bfloat16)
            left, right = first_ref[...], jnp.concatenate([high, high, low], axis=0)
        else:
            left, right = first_ref[:, : 2 * ROWS], jnp.concatenate([high, high], axis=0)
        part = dot(left, right)
        re, im = turned(part[:ROWS], part[ROWS:], turn_ref)
        rows = pl.ds(pl.multiple_of(c * ROWS, ROWS), ROWS)
        mixed[rows, :COLS] = re.astype(jnp.bfloat16)
        mixed[rows, COLS:] = im.astype(jnp.bfloat16)
        return carry

    lax.fori_loop(0, CHANS, step, 0, unroll=4)
    second_stage(mixed, second_ref, out)


def product_to(mixed, left, right, conj):
    def step(i, carry):
        rows = pl.ds(pl.multiple_of(i * ROWS, ROWS), ROWS)
        lr, li = left[rows, :COLS], left[rows, COLS:]
        rr, ri = right[rows, :COLS], right[rows, COLS:]
        if conj:
            re, im = lr * rr + li * ri, li * rr - lr * ri
        else:
            re, im = lr * rr - li * ri, -(lr * ri + li * rr)
        mixed[rows, :COLS] = re.astype(jnp.bfloat16)
        mixed[rows, COLS:] = im.astype(jnp.bfloat16)
        return carry

    lax.fori_loop(0, CHANS, step, 0, unroll=2)


def signal_of(mixed, last_ref, turn_ref, second_ref, spec, grid):
    second_stage(mixed, second_ref, spec)

    def step(c, carry):
        rows = pl.ds(pl.multiple_of(c * ROWS, ROWS), ROWS)
        re, im = turned(spec[rows, :COLS], spec[rows, COLS:], turn_ref)
        both = jnp.concatenate([re, im], axis=0)
        high = both.astype(jnp.bfloat16)
        low = (both - high.astype(jnp.float32)).astype(jnp.bfloat16)
        signal = dot(last_ref[...], jnp.concatenate([high, low], axis=0))
        for half in range(2):
            grid[half, pl.ds(c, ROWS, stride=CHANS), :] = signal[:, half * LANES : (half + 1) * LANES]
        return carry

    lax.fori_loop(0, CHANS, step, 0, unroll=4)


def give_blocks(grid, blocks_ref):
    def step(s, carry):
        for part in range(4):
            rows = pl.ds(pl.multiple_of(s * 32 + part // 2 * CHANS, CHANS), CHANS)
            blocks_ref[s, :, part * LANES : (part + 1) * LANES] = grid[part % 2, rows, :].astype(jnp.bfloat16)
        return carry

    lax.fori_loop(0, SEQ_BLOCKS, step, 0, unroll=4)


def conv_kernel(
    gated_ref, taps_ref, skip_ref, first_ref, last_ref, turn_ref, second_ref,
    conv_ref, taps_spec, gated_spec, grid, mixed, spec,
):
    for a in range(ROWS):
        for half in range(2):
            start = a * COLS + half * LANES
            grid[half, a * CHANS : (a + 1) * CHANS, :] = taps_ref[:, start : start + LANES]
    lane = lax.broadcasted_iota(jnp.int32, (CHANS, LANES), 1)
    grid[0, :CHANS, :] += jnp.where(lane == 0, skip_ref[...], 0.0)
    spectrum_of(grid, first_ref, turn_ref, second_ref, mixed, taps_spec, True)
    take_blocks(gated_ref, grid)
    spectrum_of(grid, first_ref, turn_ref, second_ref, mixed, gated_spec, False)
    product_to(mixed, taps_spec, gated_spec, False)
    signal_of(mixed, last_ref, turn_ref, second_ref, spec, grid)
    give_blocks(grid, conv_ref)


def grad_kernel(
    grad_ref, gated_ref, taps_spec, gated_spec, first_ref, last_ref, turn_ref, second_ref,
    back_ref, taps_grad_ref, skip_grad_ref, grid, mixed, spec, grad_spec,
):
    take_blocks(grad_ref, grid)
    spectrum_of(grid, first_ref, turn_ref, second_ref, mixed, grad_spec, False)
    product_to(mixed, taps_spec, grad_spec, True)
    signal_of(mixed, last_ref, turn_ref, second_ref, spec, grid)
    give_blocks(grid, back_ref)
    product_to(mixed, gated_spec, grad_spec, True)
    signal_of(mixed, last_ref, turn_ref, second_ref, spec, grid)
    for a in range(ROWS):
        for half in range(2):
            start = a * COLS + half * LANES
            taps_grad_ref[:, start : start + LANES] = grid[half, a * CHANS : (a + 1) * CHANS, :]

    def step(s, total):
        return total + grad_ref[s].astype(jnp.float32) * gated_ref[s].astype(jnp.float32)

    total = lax.fori_loop(0, SEQ_BLOCKS, step, jnp.zeros((CHANS, 2 * COLS), jnp.float32))
    skip_grad_ref[...] = jnp.sum(total, axis=1, keepdims=True)


def vmem_specs(count):
    return [pl.BlockSpec(memory_space=pltpu.VMEM)] * count


def body(query_gate, key_branch, value_branch, filter_taps, skip_gain, out_weight, out_grad):
    first, last, turn, second = [jnp.asarray(t) for t in tables()]
    full_grad = lax.all_gather(out_grad, "tp", axis=1, tiled=True)
    query_f = query_gate.astype(jnp.float32)
    key_f = key_branch.astype(jnp.float32)
    value_f = value_branch.astype(jnp.float32)
    blocks = (SEQ_BLOCKS, CHANS, 2 * COLS)
    spec_shape = jax.ShapeDtypeStruct((CHANS * ROWS, 2 * COLS), jnp.float32)
    grid = pltpu.VMEM((2, CHANS * ROWS, LANES), jnp.float32)
    mixed_s = pltpu.VMEM((CHANS * ROWS, 2 * COLS), jnp.bfloat16)
    spec_s = pltpu.VMEM((CHANS * ROWS, 2 * COLS), jnp.float32)
    params = pltpu.CompilerParams(vmem_limit_bytes=40 * 1024 * 1024)

    gated = (key_f * value_f).astype(jnp.bfloat16)
    gated_chan = lax.all_to_all(gated.reshape(blocks), "ctx", split_axis=0, concat_axis=0)
    conv_chan, taps_spec, gated_spec = pl.pallas_call(
        conv_kernel,
        out_shape=(jax.ShapeDtypeStruct(blocks, jnp.bfloat16), spec_shape, spec_shape),
        in_specs=vmem_specs(7),
        out_specs=vmem_specs(3),
        scratch_shapes=[grid, mixed_s, spec_s],
        compiler_params=params,
    )(gated_chan, filter_taps, skip_gain[:, None], first, last, turn, second)
    conv_out = lax.all_to_all(conv_chan, "ctx", split_axis=0, concat_axis=0).reshape(query_gate.shape)
    conv_f = conv_out.astype(jnp.float32)
    grad_mixed = lax.dot_general(
        out_weight, full_grad, (((1,), (1,)), ((), ())), preferred_element_type=jnp.float32
    )
    grad_conv = (grad_mixed * query_f).astype(jnp.bfloat16)
    grad_chan = lax.all_to_all(grad_conv.reshape(blocks), "ctx", split_axis=0, concat_axis=0)
    mixed = (query_f * conv_f).astype(jnp.bfloat16)
    terms = lax.dot_general(mixed, full_grad, (((1,), (0,)), ((), ())), preferred_element_type=jnp.float32)
    terms = terms.astype(jnp.bfloat16).reshape(terms.shape[0], SEQ_BLOCKS, -1).transpose(1, 0, 2)
    terms = lax.all_to_all(terms, "ctx", split_axis=0, concat_axis=0)
    grad_weight = jnp.sum(terms.astype(jnp.float32), axis=0)
    back_chan, grad_filter, grad_skip = pl.pallas_call(
        grad_kernel,
        out_shape=(
            jax.ShapeDtypeStruct(blocks, jnp.bfloat16),
            jax.ShapeDtypeStruct(filter_taps.shape, jnp.float32),
            jax.ShapeDtypeStruct((CHANS, 1), jnp.float32),
        ),
        in_specs=vmem_specs(8),
        out_specs=vmem_specs(3),
        scratch_shapes=[grid, mixed_s, spec_s, spec_s],
        compiler_params=params,
    )(grad_chan, gated_chan, taps_spec, gated_spec, first, last, turn, second)
    grad_gated = lax.all_to_all(back_chan, "ctx", split_axis=0, concat_axis=0).reshape(query_gate.shape)
    grad_query = (grad_mixed * conv_f).astype(jnp.bfloat16)
    grad_gated_f = grad_gated.astype(jnp.float32)
    grad_key = (grad_gated_f * value_f).astype(jnp.bfloat16)
    grad_value = (grad_gated_f * key_f).astype(jnp.bfloat16)
    return (grad_query, grad_key, grad_value, grad_filter, grad_skip[:, 0], grad_weight)


def solution(mesh):
    placed = (
        P("tp", "ctx"),
        P("tp", "ctx"),
        P("tp", "ctx"),
        P(("tp", "ctx"), None),
        P(("tp", "ctx")),
        P("tp", None),
        P("ctx", "tp"),
    )
    return jax.shard_map(
        body,
        mesh=mesh,
        in_specs=placed,
        out_specs=(
            P("tp", "ctx"),
            P("tp", "ctx"),
            P("tp", "ctx"),
            P(("tp", "ctx"), None),
            P(("tp", "ctx")),
            P("tp", "ctx"),
        ),
        check_vma=False,
    )
```

```python
import numpy as np
import ml_dtypes
import jax
import jax.numpy as jnp
from jax import lax
from jax.experimental import pallas as pl
from jax.experimental.pallas import tpu as pltpu
from jax.sharding import PartitionSpec as P

ROWS = 64
COLS = 256
LANES = 128
CHANS = 16
SEQ_BLOCKS = 32
COT_CHUNKS = 4
COT_ROWS = 128


def bf16_pair(values):
    high = values.astype(ml_dtypes.bfloat16)
    low = (values - high.astype(np.float64)).astype(ml_dtypes.bfloat16)
    return high, low


def tables():
    ka = np.arange(ROWS) + 0.5
    phase_a = 2.0 * np.pi * np.outer(ka, np.arange(ROWS)) / (2 * ROWS)
    first = np.concatenate([np.cos(phase_a), -np.sin(phase_a)], axis=0)
    high, low = bf16_pair(first)
    first = np.concatenate([high, low, high], axis=1)
    last = np.concatenate([np.cos(phase_a).T, np.sin(phase_a).T], axis=1) / (ROWS * COLS)
    last = last.astype(ml_dtypes.bfloat16)
    last = np.concatenate([last, last], axis=1)
    phase_t = 2.0 * np.pi * np.outer(ka, np.arange(COLS)) / (2 * ROWS * COLS)
    turn = np.concatenate([np.cos(phase_t), np.sin(phase_t)], axis=1).astype(np.float32)
    phase_b = 2.0 * np.pi * (np.outer(np.arange(COLS), np.arange(COLS)) % COLS) / COLS
    cos_b, sin_b = np.cos(phase_b), np.sin(phase_b)
    second = np.block([[cos_b, -sin_b], [sin_b, cos_b]]).astype(ml_dtypes.bfloat16)
    return first, last, turn, second


def dot(left, right):
    return jnp.dot(left, right, preferred_element_type=jnp.float32)


def turned(re, im, turn_ref):
    cos, sin = turn_ref[:, :COLS], turn_ref[:, COLS:]
    return re * cos + im * sin, im * cos - re * sin


def take_blocks(blocks_ref, grid):
    def step(s, carry):
        block = blocks_ref[s].astype(jnp.float32)
        for part in range(4):
            rows = pl.ds(pl.multiple_of(s * 32 + part // 2 * CHANS, CHANS), CHANS)
            grid[part % 2, rows, :] = block[:, part * LANES : (part + 1) * LANES]
        return carry

    lax.fori_loop(0, SEQ_BLOCKS, step, 0, unroll=4)


def second_stage(mixed, second_ref, out):
    def step(i, carry):
        rows = pl.ds(pl.multiple_of(i * 256, 256), 256)
        out[rows, :] = dot(mixed[rows, :], second_ref[...])
        return carry

    lax.fori_loop(0, CHANS * ROWS // 256, step, 0)


def spectrum_of(grid, first_ref, turn_ref, second_ref, mixed, out, wide):
    def step(c, carry):
        rows = pl.ds(c, ROWS, stride=CHANS)
        signal = jnp.concatenate([grid[0, rows, :], grid[1, rows, :]], axis=1)
        high = signal.astype(jnp.bfloat16)
        if wide:
            low = (signal - high.astype(jnp.float32)).astype(jnp.bfloat16)
            left, right = first_ref[...], jnp.concatenate([high, high, low], axis=0)
        else:
            left, right = first_ref[:, : 2 * ROWS], jnp.concatenate([high, high], axis=0)
        part = dot(left, right)
        re, im = turned(part[:ROWS], part[ROWS:], turn_ref)
        rows = pl.ds(pl.multiple_of(c * ROWS, ROWS), ROWS)
        mixed[rows, :COLS] = re.astype(jnp.bfloat16)
        mixed[rows, COLS:] = im.astype(jnp.bfloat16)
        return carry

    lax.fori_loop(0, CHANS, step, 0, unroll=4)
    second_stage(mixed, second_ref, out)


def product_to(mixed, left, right, conj):
    def step(i, carry):
        rows = pl.ds(pl.multiple_of(i * ROWS, ROWS), ROWS)
        lr, li = left[rows, :COLS], left[rows, COLS:]
        rr, ri = right[rows, :COLS], right[rows, COLS:]
        if conj:
            re, im = lr * rr + li * ri, li * rr - lr * ri
        else:
            re, im = lr * rr - li * ri, -(lr * ri + li * rr)
        mixed[rows, :COLS] = re.astype(jnp.bfloat16)
        mixed[rows, COLS:] = im.astype(jnp.bfloat16)
        return carry

    lax.fori_loop(0, CHANS, step, 0, unroll=2)


def signal_of(mixed, last_ref, turn_ref, second_ref, spec, grid):
    second_stage(mixed, second_ref, spec)

    def step(c, carry):
        rows = pl.ds(pl.multiple_of(c * ROWS, ROWS), ROWS)
        re, im = turned(spec[rows, :COLS], spec[rows, COLS:], turn_ref)
        both = jnp.concatenate([re, im], axis=0)
        high = both.astype(jnp.bfloat16)
        low = (both - high.astype(jnp.float32)).astype(jnp.bfloat16)
        signal = dot(last_ref[...], jnp.concatenate([high, low], axis=0))
        for half in range(2):
            grid[half, pl.ds(c, ROWS, stride=CHANS), :] = signal[:, half * LANES : (half + 1) * LANES]
        return carry

    lax.fori_loop(0, CHANS, step, 0, unroll=4)


def give_blocks(grid, blocks_ref):
    def step(s, carry):
        for part in range(4):
            rows = pl.ds(pl.multiple_of(s * 32 + part // 2 * CHANS, CHANS), CHANS)
            blocks_ref[s, :, part * LANES : (part + 1) * LANES] = grid[part % 2, rows, :].astype(jnp.bfloat16)
        return carry

    lax.fori_loop(0, SEQ_BLOCKS, step, 0, unroll=4)


def taps_to_grid(taps, skip_ref, grid):
    for a in range(ROWS):
        for half in range(2):
            start = a * COLS + half * LANES
            grid[half, a * CHANS : (a + 1) * CHANS, :] = taps[:, start : start + LANES]
    row = lax.broadcasted_iota(jnp.int32, (CHANS, CHANS), 0)
    col = lax.broadcasted_iota(jnp.int32, (CHANS, CHANS), 1)
    skip = jnp.sum(jnp.where(row == col, skip_ref[...], 0.0), axis=1, keepdims=True)
    lane = lax.broadcasted_iota(jnp.int32, (CHANS, LANES), 1)
    grid[0, :CHANS, :] += jnp.where(lane == 0, skip, 0.0)


def grid_to_taps(grid, taps):
    for a in range(ROWS):
        for half in range(2):
            start = a * COLS + half * LANES
            taps[:, start : start + LANES] = grid[half, a * CHANS : (a + 1) * CHANS, :]


def skip_gradient(grad, gated, out_ref):
    def step(s, total):
        return total + grad[s].astype(jnp.float32) * gated[s].astype(jnp.float32)

    total = lax.fori_loop(0, SEQ_BLOCKS, step, jnp.zeros((CHANS, 2 * COLS), jnp.float32))
    total = jnp.sum(total, axis=1, keepdims=True)
    row = lax.broadcasted_iota(jnp.int32, (CHANS, CHANS), 0)
    col = lax.broadcasted_iota(jnp.int32, (CHANS, CHANS), 1)
    out_ref[...] = jnp.sum(jnp.where(row == col, total, 0.0), axis=0, keepdims=True)


def for_blocks(step, unroll=4):
    def body(s, carry):
        step(s)
        return carry

    lax.fori_loop(0, SEQ_BLOCKS, body, 0, unroll=unroll)


def block_rows(s):
    return pl.ds(pl.multiple_of(s * CHANS, CHANS), CHANS)


def kernel(
    query_in, key_in, value_in, taps_in, skip_ref, weight_in, cot_in, first_in, last_in, turn_in, second_in,
    query_out, key_out, value_out, taps_out, skip_out, weight_out,
    query, key, value, taps, weight, first, last, turn, second,
    cot, gated, gated_got, conv, conv_got, grad, grad_got, back, back_got, terms, terms_got, grad_mixed, gate_mixed,
    grid, mixed, spec, taps_spec, gated_spec, grad_spec, query_res, key_res, value_res, taps_res, weight_res,
    load_sem, store_sem, gated_sems, conv_sems, grad_sems, back_sems, terms_sems, near_sems, far_sems, relay_sems,
):
    me = lax.axis_index("ctx")
    part = lax.axis_index("tp")
    sibling = part + 1 - 2 * (part % 2)
    across = (part + 2) % 4
    diagonal = (sibling + 2) % 4

    def load(index, source, target):
        copy = pltpu.make_async_copy(source, target, load_sem.at[index])
        copy.start()
        return copy

    key_load = load(0, key_in, key)
    value_load = load(1, value_in, value)
    cot_load = load(2, cot_in, cot.at[part])
    first_load = load(3, first_in, first)
    turn_load = load(4, turn_in, turn)
    second_load = load(5, second_in, second)
    taps_load = load(6, taps_in, taps)
    last_load = load(7, last_in, last)
    weight_load = load(8, weight_in, weight)
    query_load = load(9, query_in, query)

    barrier = pltpu.get_barrier_semaphore()

    def greet(i, carry):
        pl.semaphore_signal(
            barrier, inc=1, device_id={"ctx": (me + i) % SEQ_BLOCKS}, device_id_type=pl.DeviceIdType.MESH
        )
        return carry

    lax.fori_loop(1, SEQ_BLOCKS, greet, 0)
    for other in (sibling, across):
        pl.semaphore_signal(barrier, inc=1, device_id={"tp": other}, device_id_type=pl.DeviceIdType.MESH)

    key_load.wait()
    value_load.wait()

    def gate(s):
        gated[s] = (key[s].astype(jnp.float32) * value[s].astype(jnp.float32)).astype(jnp.bfloat16)

    for_blocks(gate)
    pl.semaphore_wait(barrier, SEQ_BLOCKS + 1)

    def to_peer(source, target, sems, peer, slot):
        return pltpu.make_async_remote_copy(
            src_ref=source.at[peer],
            dst_ref=target.at[slot],
            send_sem=sems.at[0, peer],
            recv_sem=sems.at[1, slot],
            device_id={"ctx": peer},
            device_id_type=pl.DeviceIdType.MESH,
        )

    def exchange(source, target, sems):
        def step(i, carry):
            to_peer(source, target, sems, (me + i) % SEQ_BLOCKS, me).start()
            return carry

        lax.fori_loop(1, SEQ_BLOCKS, step, 0)
        target[me] = source[me]

    def arrived(source, target, sems):
        def step(i, carry):
            peer = (me + SEQ_BLOCKS - i) % SEQ_BLOCKS
            to_peer(source, target, sems, peer, peer).wait_recv()
            return carry

        lax.fori_loop(1, SEQ_BLOCKS, step, 0)

    def sent(source, target, sems):
        def step(i, carry):
            to_peer(source, target, sems, (me + i) % SEQ_BLOCKS, me).wait_send()
            return carry

        lax.fori_loop(1, SEQ_BLOCKS, step, 0)

    exchange(gated, gated_got, gated_sems)

    near = pltpu.make_async_remote_copy(
        src_ref=cot_in,
        dst_ref=cot.at[part],
        send_sem=near_sems.at[0],
        recv_sem=near_sems.at[1],
        device_id={"tp": sibling},
        device_id_type=pl.DeviceIdType.MESH,
    )
    near.start()

    def chunk_rows(j):
        return pl.ds(j * COT_ROWS, COT_ROWS)

    def far(j):
        return pltpu.make_async_remote_copy(
            src_ref=cot_in.at[chunk_rows(j)],
            dst_ref=cot.at[part, chunk_rows(j)],
            send_sem=far_sems.at[0, j],
            recv_sem=far_sems.at[1, j],
            device_id={"tp": across},
            device_id_type=pl.DeviceIdType.MESH,
        )

    def relay(j):
        return pltpu.make_async_remote_copy(
            src_ref=cot.at[across, chunk_rows(j)],
            dst_ref=cot.at[across, chunk_rows(j)],
            send_sem=relay_sems.at[0, j],
            recv_sem=relay_sems.at[1, j],
            device_id={"tp": sibling},
            device_id_type=pl.DeviceIdType.MESH,
        )

    for j in range(COT_CHUNKS):
        far(j).start()

    taps_load.wait()
    first_load.wait()
    turn_load.wait()
    second_load.wait()
    taps_to_grid(taps, skip_ref, grid)
    spectrum_of(grid, first, turn, second, mixed, taps_spec, True)

    def mix_features(p, fresh):
        def step(i, carry):
            rows = pl.ds(pl.multiple_of(i * 256, 256), 256)
            columns = pl.ds(pl.multiple_of(p * 1024, 1024), 1024)
            term = lax.dot_general(
                weight[:, columns], cot[p, rows, :], (((1,), (1,)), ((), ())),
                preferred_element_type=jnp.float32,
            )
            if fresh:
                grad_mixed[:, rows] = term
            else:
                grad_mixed[:, rows] += term
            return carry

        lax.fori_loop(0, 2, step, 0)

    cot_load.wait()
    weight_load.wait()
    mix_features(part, True)
    last_load.wait()
    query_load.wait()

    arrived(gated, gated_got, gated_sems)
    take_blocks(gated_got, grid)
    spectrum_of(grid, first, turn, second, mixed, gated_spec, False)
    product_to(mixed, taps_spec, gated_spec, False)
    signal_of(mixed, last, turn, second, spec, grid)
    give_blocks(grid, conv)
    exchange(conv, conv_got, conv_sems)

    near.wait_recv()
    mix_features(sibling, False)
    for j in range(COT_CHUNKS):
        far(j).wait_recv()
        relay(j).start()
    mix_features(across, False)
    for j in range(COT_CHUNKS):
        relay(j).wait_recv()
    mix_features(diagonal, False)

    def cotangent(s):
        grad[s] = (grad_mixed[block_rows(s), :] * query[s].astype(jnp.float32)).astype(jnp.bfloat16)

    for_blocks(cotangent)
    exchange(grad, grad_got, grad_sems)

    arrived(conv, conv_got, conv_sems)

    def gate_output(s):
        conv_f = conv_got[s].astype(jnp.float32)
        gate_mixed[block_rows(s), :] = (query[s].astype(jnp.float32) * conv_f).astype(jnp.bfloat16)
        query_res[s] = (grad_mixed[block_rows(s), :] * conv_f).astype(jnp.bfloat16)

    for_blocks(gate_output)
    query_store = pltpu.make_async_copy(query_res, query_out, store_sem.at[0])
    query_store.start()

    def term_step(i, carry):
        pair = (me // 2 + 1 + i) % (SEQ_BLOCKS // 2)
        columns = pl.ds(pl.multiple_of(pair % 4 * 256, 256), 256)
        term = dot(gate_mixed[...], cot[pair // 4, :, columns]).astype(jnp.bfloat16)
        for half in range(2):
            peer = pair * 2 + half
            terms[peer] = term[:, half * LANES : (half + 1) * LANES]

            @pl.when(peer != me)
            def _():
                to_peer(terms, terms_got, terms_sems, peer, me).start()

        return carry

    lax.fori_loop(0, SEQ_BLOCKS // 2, term_step, 0)

    arrived(grad, grad_got, grad_sems)
    take_blocks(grad_got, grid)
    spectrum_of(grid, first, turn, second, mixed, grad_spec, False)
    product_to(mixed, taps_spec, grad_spec, True)
    signal_of(mixed, last, turn, second, spec, grid)
    give_blocks(grid, back)
    exchange(back, back_got, back_sems)
    product_to(mixed, gated_spec, grad_spec, True)
    signal_of(mixed, last, turn, second, spec, grid)
    grid_to_taps(grid, taps_res)
    taps_store = pltpu.make_async_copy(taps_res, taps_out, store_sem.at[1])
    taps_store.start()
    skip_gradient(grad_got, gated_got, skip_out)

    weight_res[...] = terms[me].astype(jnp.float32)

    def sum_step(i, carry):
        peer = (me + SEQ_BLOCKS - i) % SEQ_BLOCKS
        to_peer(terms, terms_got, terms_sems, peer, peer).wait_recv()
        weight_res[...] += terms_got[peer].astype(jnp.float32)
        return carry

    arrived(back, back_got, back_sems)

    def gate_input(s):
        back_f = back_got[s].astype(jnp.float32)
        key_res[s] = (back_f * value[s].astype(jnp.float32)).astype(jnp.bfloat16)
        value_res[s] = (back_f * key[s].astype(jnp.float32)).astype(jnp.bfloat16)

    for_blocks(gate_input)
    key_store = pltpu.make_async_copy(key_res, key_out, store_sem.at[2])
    key_store.start()
    value_store = pltpu.make_async_copy(value_res, value_out, store_sem.at[3])
    value_store.start()
    lax.fori_loop(1, SEQ_BLOCKS, sum_step, 0)
    weight_store = pltpu.make_async_copy(weight_res, weight_out, store_sem.at[4])
    weight_store.start()

    sent(gated, gated_got, gated_sems)
    sent(conv, conv_got, conv_sems)
    sent(grad, grad_got, grad_sems)
    sent(back, back_got, back_sems)
    sent(terms, terms_got, terms_sems)
    near.wait_send()
    for j in range(COT_CHUNKS):
        far(j).wait_send()
        relay(j).wait_send()
    for copy in (query_store, taps_store, key_store, value_store, weight_store):
        copy.wait()


def body(query_gate, key_branch, value_branch, filter_taps, skip_gain, out_weight, out_grad):
    constants = [jnp.asarray(t) for t in tables()]
    blocks = (SEQ_BLOCKS, CHANS, 2 * COLS)
    bf16, f32 = jnp.bfloat16, jnp.float32
    in_hbm = pl.BlockSpec(memory_space=pl.ANY)
    in_vmem = pl.BlockSpec(memory_space=pltpu.VMEM)
    block_buffer = pltpu.VMEM(blocks, bf16)
    spec_buffer = pltpu.VMEM((CHANS * ROWS, 2 * COLS), f32)
    terms_buffer = pltpu.VMEM((SEQ_BLOCKS, 512, LANES), bf16)
    peer_sems = pltpu.SemaphoreType.DMA((2, SEQ_BLOCKS))
    dma = pltpu.SemaphoreType.DMA
    grad_query, grad_key, grad_value, grad_filter, grad_skip, grad_weight = pl.pallas_call(
        kernel,
        out_shape=(
            jax.ShapeDtypeStruct(blocks, bf16),
            jax.ShapeDtypeStruct(blocks, bf16),
            jax.ShapeDtypeStruct(blocks, bf16),
            jax.ShapeDtypeStruct(filter_taps.shape, f32),
            jax.ShapeDtypeStruct((1, CHANS), f32),
            jax.ShapeDtypeStruct((512, LANES), f32),
        ),
        in_specs=[in_hbm] * 4 + [in_vmem] + [in_hbm] * 6,
        out_specs=[in_hbm] * 4 + [in_vmem, in_hbm],
        scratch_shapes=[
            block_buffer, block_buffer, block_buffer,
            pltpu.VMEM(filter_taps.shape, f32),
            pltpu.VMEM(out_weight.shape, bf16),
            *[pltpu.VMEM(t.shape, t.dtype) for t in constants],
            pltpu.VMEM((4, 512, 1024), bf16),
            *[block_buffer] * 8,
            terms_buffer, terms_buffer,
            pltpu.VMEM((512, 512), f32),
            pltpu.VMEM((512, 512), bf16),
            pltpu.VMEM((2, CHANS * ROWS, LANES), f32),
            pltpu.VMEM((CHANS * ROWS, 2 * COLS), bf16),
            *[spec_buffer] * 4,
            block_buffer, block_buffer, block_buffer,
            pltpu.VMEM(filter_taps.shape, f32),
            pltpu.VMEM((512, LANES), f32),
            dma((10,)), dma((5,)),
            *[peer_sems] * 5,
            dma((2,)), dma((2, COT_CHUNKS)), dma((2, COT_CHUNKS)),
        ],
        compiler_params=pltpu.CompilerParams(
            collective_id=0, has_side_effects=True, vmem_limit_bytes=56 * 1024 * 1024
        ),
    )(
        query_gate.reshape(blocks), key_branch.reshape(blocks), value_branch.reshape(blocks), filter_taps,
        skip_gain[None, :], out_weight, out_grad, *constants,
    )
    shape = query_gate.shape
    return (
        grad_query.reshape(shape), grad_key.reshape(shape), grad_value.reshape(shape),
        grad_filter, grad_skip[0], grad_weight,
    )


def solution(mesh):
    placed = (
        P("tp", "ctx"),
        P("tp", "ctx"),
        P("tp", "ctx"),
        P(("tp", "ctx"), None),
        P(("tp", "ctx")),
        P("tp", None),
        P("ctx", "tp"),
    )
    return jax.shard_map(
        body,
        mesh=mesh,
        in_specs=placed,
        out_specs=(
            P("tp", "ctx"),
            P("tp", "ctx"),
            P("tp", "ctx"),
            P(("tp", "ctx"), None),
            P(("tp", "ctx")),
            P("tp", "ctx"),
        ),
        check_vma=False,
    )
```

```python
import numpy as np
import ml_dtypes
import jax
import jax.numpy as jnp
from jax import lax
from jax.experimental import pallas as pl
from jax.experimental.pallas import tpu as pltpu
from jax.sharding import PartitionSpec as P

ROWS = 64
COLS = 256
LANES = 128
CHANS = 16
SEQ_BLOCKS = 32
COT_CHUNKS = 4
COT_ROWS = 128
TERM_CHUNKS = 2
TERM_ROWS = 256 // TERM_CHUNKS


def bf16_pair(values):
    high = values.astype(ml_dtypes.bfloat16)
    low = (values - high.astype(np.float64)).astype(ml_dtypes.bfloat16)
    return high, low


def tables():
    ka = np.arange(ROWS) + 0.5
    phase_a = 2.0 * np.pi * np.outer(ka, np.arange(ROWS)) / (2 * ROWS)
    first = np.concatenate([np.cos(phase_a), -np.sin(phase_a)], axis=0)
    high, low = bf16_pair(first)
    first = np.concatenate([high, low, high], axis=1)
    last = np.concatenate([np.cos(phase_a).T, np.sin(phase_a).T], axis=1) / (ROWS * COLS)
    last = last.astype(ml_dtypes.bfloat16)
    last = np.concatenate([last, last], axis=1)
    phase_t = 2.0 * np.pi * np.outer(ka, np.arange(COLS)) / (2 * ROWS * COLS)
    turn = np.concatenate([np.cos(phase_t), np.sin(phase_t)], axis=1).astype(np.float32)
    phase_b = 2.0 * np.pi * (np.outer(np.arange(COLS), np.arange(COLS)) % COLS) / COLS
    cos_b, sin_b = np.cos(phase_b), np.sin(phase_b)
    second = np.block([[cos_b, -sin_b], [sin_b, cos_b]]).astype(ml_dtypes.bfloat16)
    return [t.astype(np.float32) for t in (first, last, turn, second)]


def dot(left, right):
    return jnp.dot(left, right, preferred_element_type=jnp.float32)


def turned(re, im, turn_ref):
    cos, sin = turn_ref[:, :COLS], turn_ref[:, COLS:]
    return re * cos + im * sin, im * cos - re * sin


def take_blocks(blocks_ref, grid):
    def step(s, carry):
        block = blocks_ref[s].astype(jnp.float32)
        for part in range(4):
            rows = pl.ds(pl.multiple_of(s * 32 + part // 2 * CHANS, CHANS), CHANS)
            grid[part % 2, rows, :] = block[:, part * LANES : (part + 1) * LANES]
        return carry

    lax.fori_loop(0, SEQ_BLOCKS, step, 0, unroll=4)


def second_stage(mixed, second_ref, out):
    def step(i, carry):
        rows = pl.ds(pl.multiple_of(i * 256, 256), 256)
        out[rows, :] = dot(mixed[rows, :], second_ref[...])
        return carry

    lax.fori_loop(0, CHANS * ROWS // 256, step, 0)


def spectrum_of(grid, first_ref, turn_ref, second_ref, mixed, out, wide):
    def step(c, carry):
        rows = pl.ds(c, ROWS, stride=CHANS)
        signal = jnp.concatenate([grid[0, rows, :], grid[1, rows, :]], axis=1)
        high = signal.astype(jnp.bfloat16)
        if wide:
            low = (signal - high.astype(jnp.float32)).astype(jnp.bfloat16)
            left, right = first_ref[...], jnp.concatenate([high, high, low], axis=0)
        else:
            left, right = first_ref[:, : 2 * ROWS], jnp.concatenate([high, high], axis=0)
        part = dot(left, right)
        re, im = turned(part[:ROWS], part[ROWS:], turn_ref)
        rows = pl.ds(pl.multiple_of(c * ROWS, ROWS), ROWS)
        mixed[rows, :COLS] = re.astype(jnp.bfloat16)
        mixed[rows, COLS:] = im.astype(jnp.bfloat16)
        return carry

    lax.fori_loop(0, CHANS, step, 0, unroll=4)
    second_stage(mixed, second_ref, out)


def product_to(mixed, left, right, conj):
    def step(i, carry):
        rows = pl.ds(pl.multiple_of(i * ROWS, ROWS), ROWS)
        lr, li = left[rows, :COLS], left[rows, COLS:]
        rr, ri = right[rows, :COLS], right[rows, COLS:]
        if conj:
            re, im = lr * rr + li * ri, li * rr - lr * ri
        else:
            re, im = lr * rr - li * ri, -(lr * ri + li * rr)
        mixed[rows, :COLS] = re.astype(jnp.bfloat16)
        mixed[rows, COLS:] = im.astype(jnp.bfloat16)
        return carry

    lax.fori_loop(0, CHANS, step, 0, unroll=2)


def signal_of(mixed, last_ref, turn_ref, second_ref, spec, grid):
    second_stage(mixed, second_ref, spec)

    def step(c, carry):
        rows = pl.ds(pl.multiple_of(c * ROWS, ROWS), ROWS)
        re, im = turned(spec[rows, :COLS], spec[rows, COLS:], turn_ref)
        both = jnp.concatenate([re, im], axis=0)
        high = both.astype(jnp.bfloat16)
        low = (both - high.astype(jnp.float32)).astype(jnp.bfloat16)
        signal = dot(last_ref[...], jnp.concatenate([high, low], axis=0))
        for half in range(2):
            grid[half, pl.ds(c, ROWS, stride=CHANS), :] = signal[:, half * LANES : (half + 1) * LANES]
        return carry

    lax.fori_loop(0, CHANS, step, 0, unroll=4)


def give_blocks(grid, blocks_ref):
    def step(s, carry):
        for part in range(4):
            rows = pl.ds(pl.multiple_of(s * 32 + part // 2 * CHANS, CHANS), CHANS)
            blocks_ref[s, :, part * LANES : (part + 1) * LANES] = grid[part % 2, rows, :].astype(jnp.bfloat16)
        return carry

    lax.fori_loop(0, SEQ_BLOCKS, step, 0, unroll=4)


def taps_to_grid(taps, skip_ref, grid):
    for a in range(ROWS):
        for half in range(2):
            start = a * COLS + half * LANES
            grid[half, a * CHANS : (a + 1) * CHANS, :] = taps[:, start : start + LANES]
    row = lax.broadcasted_iota(jnp.int32, (CHANS, CHANS), 0)
    col = lax.broadcasted_iota(jnp.int32, (CHANS, CHANS), 1)
    skip = jnp.sum(jnp.where(row == col, skip_ref[...], 0.0), axis=1, keepdims=True)
    lane = lax.broadcasted_iota(jnp.int32, (CHANS, LANES), 1)
    grid[0, :CHANS, :] += jnp.where(lane == 0, skip, 0.0)


def grid_to_taps(grid, taps):
    for a in range(ROWS):
        for half in range(2):
            start = a * COLS + half * LANES
            taps[:, start : start + LANES] = grid[half, a * CHANS : (a + 1) * CHANS, :]


def skip_gradient(grad, gated, out_ref):
    def step(s, total):
        return total + grad[s].astype(jnp.float32) * gated[s].astype(jnp.float32)

    total = lax.fori_loop(0, SEQ_BLOCKS, step, jnp.zeros((CHANS, 2 * COLS), jnp.float32))
    total = jnp.sum(total, axis=1, keepdims=True)
    row = lax.broadcasted_iota(jnp.int32, (CHANS, CHANS), 0)
    col = lax.broadcasted_iota(jnp.int32, (CHANS, CHANS), 1)
    out_ref[...] = jnp.sum(jnp.where(row == col, total, 0.0), axis=0, keepdims=True)


def for_blocks(step, unroll=4):
    def body(s, carry):
        step(s)
        return carry

    lax.fori_loop(0, SEQ_BLOCKS, body, 0, unroll=unroll)


def block_rows(s):
    return pl.ds(pl.multiple_of(s * CHANS, CHANS), CHANS)


def kernel(
    query_in, key_in, value_in, taps_in, skip_ref, weight_in, cot_in, first_in, last_in, turn_in, second_in,
    query_out, key_out, value_out, taps_out, skip_out, weight_out,
    query, key, value, taps, weight, first_wide, last_wide, turn, second_wide, first, last, second,
    cot, gated, gated_got, conv, conv_got, grad, grad_got, back, back_got, terms, terms_got,
    second_terms, second_got, third, third_got, grad_mixed, gate_mixed,
    grid, mixed, spec, taps_spec, gated_spec, grad_spec, query_res, key_res, value_res, taps_res, weight_res,
    load_sem, store_sem, gated_sems, conv_sems, grad_sems, back_sems, terms_sems, second_sems, third_sems, near_sems, far_sems, relay_sems,
):
    me = lax.axis_index("ctx")
    part = lax.axis_index("tp")
    sibling = part + 1 - 2 * (part % 2)
    across = (part + 2) % 4
    diagonal = (sibling + 2) % 4

    def load(index, source, target):
        copy = pltpu.make_async_copy(source, target, load_sem.at[index])
        copy.start()
        return copy

    key_load = load(0, key_in, key)
    value_load = load(1, value_in, value)
    cot_load = load(2, cot_in, cot.at[part])
    first_load = load(3, first_in, first_wide)
    turn_load = load(4, turn_in, turn)
    second_load = load(5, second_in, second_wide)
    taps_load = load(6, taps_in, taps)
    last_load = load(7, last_in, last_wide)
    weight_load = load(8, weight_in, weight)
    query_load = load(9, query_in, query)

    barrier = pltpu.get_barrier_semaphore()

    def greet(i, carry):
        pl.semaphore_signal(
            barrier, inc=1, device_id={"ctx": (me + i) % SEQ_BLOCKS}, device_id_type=pl.DeviceIdType.MESH
        )
        return carry

    lax.fori_loop(1, SEQ_BLOCKS, greet, 0)
    for other in (sibling, across):
        pl.semaphore_signal(barrier, inc=1, device_id={"tp": other}, device_id_type=pl.DeviceIdType.MESH)

    key_load.wait()
    value_load.wait()

    def gate(s):
        gated[s] = (key[s].astype(jnp.float32) * value[s].astype(jnp.float32)).astype(jnp.bfloat16)

    for_blocks(gate)
    pl.semaphore_wait(barrier, SEQ_BLOCKS + 1)

    def to_device(source, target, send_sem, recv_sem, device):
        return pltpu.make_async_remote_copy(
            src_ref=source,
            dst_ref=target,
            send_sem=send_sem,
            recv_sem=recv_sem,
            device_id=device,
            device_id_type=pl.DeviceIdType.MESH,
        )

    def exchange(source, target, sems):
        def step(i, carry):
            peer = (me + i) % SEQ_BLOCKS
            to_device(source.at[peer], target.at[me], sems.at[0], sems.at[1], {"ctx": peer}).start()
            return carry

        lax.fori_loop(1, SEQ_BLOCKS, step, 0)
        target[me] = source[me]

    def whole_exchange(source, target, sems):
        blocks = pl.ds(0, SEQ_BLOCKS - 1)
        return to_device(source.at[blocks], target.at[blocks], sems.at[0], sems.at[1], {"tp": across})

    def arrived(source, target, sems):
        whole_exchange(source, target, sems).wait_recv()

    def sent(source, target, sems):
        whole_exchange(source, target, sems).wait_send()

    exchange(gated, gated_got, gated_sems)

    near = pltpu.make_async_remote_copy(
        src_ref=cot_in,
        dst_ref=cot.at[part],
        send_sem=near_sems.at[0],
        recv_sem=near_sems.at[1],
        device_id={"tp": sibling},
        device_id_type=pl.DeviceIdType.MESH,
    )
    near.start()

    def chunk_rows(j):
        return pl.ds(j * COT_ROWS, COT_ROWS)

    def far(j):
        return pltpu.make_async_remote_copy(
            src_ref=cot_in.at[chunk_rows(j)],
            dst_ref=cot.at[part, chunk_rows(j)],
            send_sem=far_sems.at[0, j],
            recv_sem=far_sems.at[1, j],
            device_id={"tp": across},
            device_id_type=pl.DeviceIdType.MESH,
        )

    def relay(j):
        return pltpu.make_async_remote_copy(
            src_ref=cot.at[across, chunk_rows(j)],
            dst_ref=cot.at[across, chunk_rows(j)],
            send_sem=relay_sems.at[0, j],
            recv_sem=relay_sems.at[1, j],
            device_id={"tp": sibling},
            device_id_type=pl.DeviceIdType.MESH,
        )

    for j in range(COT_CHUNKS):
        far(j).start()

    taps_load.wait()
    first_load.wait()
    turn_load.wait()
    second_load.wait()
    first[...] = first_wide[...].astype(jnp.bfloat16)
    second[...] = second_wide[...].astype(jnp.bfloat16)
    taps_to_grid(taps, skip_ref, grid)
    spectrum_of(grid, first, turn, second, mixed, taps_spec, True)

    def mix_features(p, fresh):
        def step(i, carry):
            rows = pl.ds(pl.multiple_of(i * 256, 256), 256)
            columns = pl.ds(pl.multiple_of(p * 1024, 1024), 1024)
            term = lax.dot_general(
                weight[:, columns], cot[p, rows, :], (((1,), (1,)), ((), ())),
                preferred_element_type=jnp.float32,
            )
            if fresh:
                grad_mixed[:, rows] = term
            else:
                grad_mixed[:, rows] += term
            return carry

        lax.fori_loop(0, 2, step, 0)

    cot_load.wait()
    weight_load.wait()
    mix_features(part, True)
    last_load.wait()
    last[...] = last_wide[...].astype(jnp.bfloat16)
    query_load.wait()

    arrived(gated, gated_got, gated_sems)
    take_blocks(gated_got, grid)
    spectrum_of(grid, first, turn, second, mixed, gated_spec, False)
    product_to(mixed, taps_spec, gated_spec, False)
    signal_of(mixed, last, turn, second, spec, grid)
    give_blocks(grid, conv)
    exchange(conv, conv_got, conv_sems)

    near.wait_recv()
    mix_features(sibling, False)
    arrived(conv, conv_got, conv_sems)

    def gate_output(s):
        gate_mixed[block_rows(s), :] = (
            query[s].astype(jnp.float32) * conv_got[s].astype(jnp.float32)
        ).astype(jnp.bfloat16)

    for_blocks(gate_output)
    for j in range(COT_CHUNKS):
        far(j).wait_recv()
        relay(j).start()
    mix_features(across, False)
    for j in range(COT_CHUNKS):
        relay(j).wait_recv()
    mix_features(diagonal, False)

    def cotangent(s):
        grad[s] = (grad_mixed[block_rows(s), :] * query[s].astype(jnp.float32)).astype(jnp.bfloat16)

    for_blocks(cotangent)
    exchange(grad, grad_got, grad_sems)

    z, y, x = me // 8, me // 2 % 4, me % 2

    def z_peer(k):
        return (z + k) % 4

    def y_peer(k):
        return (y + k) % 4

    def peer_of(half, stage, k):
        if half == stage:
            return z_peer(k), {"ctx": z_peer(k) * 8 + y * 2 + x}, z
        return y_peer(k), {"ctx": z * 8 + y_peer(k) * 2 + x}, y

    def term_rows(j):
        return pl.ds(pl.multiple_of(j * TERM_ROWS, TERM_ROWS), TERM_ROWS)

    def one_of(half, stage, source, target, sems, j, k):
        place, device, own = peer_of(half, stage, k)
        return to_device(
            source.at[half, place, term_rows(j)], target.at[half, own, term_rows(j)],
            sems.at[0, half, j, k - 1], sems.at[1, half, j, k - 1], device,
        )

    def side_of(half, j):
        return to_device(
            third.at[half, term_rows(j)], third_got.at[half, term_rows(j)],
            third_sems.at[0, half, j], third_sems.at[1, half, j], {"ctx": me + 1 - 2 * x},
        )

    def from_peer(half, stage, source, target, sems, j, k):
        place, device, own = peer_of(half, stage, 4 - k)
        return to_device(
            source.at[half, place, term_rows(j)], target.at[half, place, term_rows(j)],
            sems.at[0, half, j, k - 1], sems.at[1, half, j, k - 1], device,
        )

    def term_chunk(j):
        def step(i, carry):
            p, q = i // 4, i % 4
            columns = pl.ds(pl.multiple_of(q * 256, 256), 256)
            targets = pl.ds(pl.multiple_of(p * 256, 256), 256)
            lower = pl.ds(pl.multiple_of(256 + j * TERM_ROWS, TERM_ROWS), TERM_ROWS)
            left = jnp.concatenate([gate_mixed[term_rows(j), :], gate_mixed[lower, :]], axis=0)
            term = dot(left, cot[p, :, columns]).astype(jnp.bfloat16)
            terms[0, p, term_rows(j), columns] = term[:TERM_ROWS]
            terms[1, q, term_rows(j), targets] = term[TERM_ROWS:]
            return carry

        lax.fori_loop(0, 16, step, 0)
        for k in (2, 1, 3):
            for half in range(2):
                one_of(half, 0, terms, terms_got, terms_sems, j, k).start()

    for j in range(TERM_CHUNKS):
        term_chunk(j)

    def query_gradient(s):
        query_res[s] = (grad_mixed[block_rows(s), :] * conv_got[s].astype(jnp.float32)).astype(jnp.bfloat16)

    for_blocks(query_gradient)
    query_store = pltpu.make_async_copy(query_res, query_out, store_sem.at[0])
    query_store.start()

    arrived(grad, grad_got, grad_sems)
    take_blocks(grad_got, grid)
    spectrum_of(grid, first, turn, second, mixed, grad_spec, False)
    product_to(mixed, taps_spec, grad_spec, True)
    signal_of(mixed, last, turn, second, spec, grid)
    give_blocks(grid, back)
    exchange(back, back_got, back_sems)
    product_to(mixed, gated_spec, grad_spec, True)
    signal_of(mixed, last, turn, second, spec, grid)
    grid_to_taps(grid, taps_res)
    taps_store = pltpu.make_async_copy(taps_res, taps_out, store_sem.at[1])
    taps_store.start()
    skip_gradient(grad_got, gated_got, skip_out)

    def summed(half, stage, held, got, j, columns):
        own = z if half == stage else y
        total = held[half, own, term_rows(j), columns].astype(jnp.float32)
        for k in (1, 2, 3):
            total += got[half, (own + k) % 4, term_rows(j), columns].astype(jnp.float32)
        return total

    for j in range(TERM_CHUNKS):
        for half in range(2):
            for k in (1, 3, 2):
                from_peer(half, 0, terms, terms_got, terms_sems, j, k).wait_recv()
            for place in range(4):
                columns = pl.ds(place * 256, 256)
                total = summed(half, 0, terms, terms_got, j, columns)
                second_terms[half, place, term_rows(j)] = total.astype(jnp.bfloat16)
            for k in (2, 1, 3):
                one_of(half, 1, second_terms, second_got, second_sems, j, k).start()

    arrived(back, back_got, back_sems)

    def gate_input(s):
        back_f = back_got[s].astype(jnp.float32)
        key_res[s] = (back_f * value[s].astype(jnp.float32)).astype(jnp.bfloat16)
        value_res[s] = (back_f * key[s].astype(jnp.float32)).astype(jnp.bfloat16)

    for_blocks(gate_input)
    key_store = pltpu.make_async_copy(key_res, key_out, store_sem.at[2])
    key_store.start()
    value_store = pltpu.make_async_copy(value_res, value_out, store_sem.at[3])
    value_store.start()
    mine = pl.ds(pl.multiple_of(x * LANES, LANES), LANES)
    others = pl.ds(pl.multiple_of((1 - x) * LANES, LANES), LANES)
    for j in range(TERM_CHUNKS):
        for half in range(2):
            for k in (1, 3, 2):
                from_peer(half, 1, second_terms, second_got, second_sems, j, k).wait_recv()
            third[half, term_rows(j)] = summed(half, 1, second_terms, second_got, j, others).astype(jnp.bfloat16)
            side_of(half, j).start()
            weight_res[pl.ds(half * 256 + j * TERM_ROWS, TERM_ROWS), :] = summed(
                half, 1, second_terms, second_got, j, mine
            )
    for j in range(TERM_CHUNKS):
        for half in range(2):
            side_of(half, j).wait_recv()
            rows = pl.ds(half * 256 + j * TERM_ROWS, TERM_ROWS)
            weight_res[rows, :] += third_got[half, term_rows(j)].astype(jnp.float32)
    weight_store = pltpu.make_async_copy(weight_res, weight_out, store_sem.at[4])
    weight_store.start()

    sent(gated, gated_got, gated_sems)
    sent(conv, conv_got, conv_sems)
    sent(grad, grad_got, grad_sems)
    sent(back, back_got, back_sems)
    for j in range(TERM_CHUNKS):
        for half in range(2):
            for k in (1, 2, 3):
                one_of(half, 0, terms, terms_got, terms_sems, j, k).wait_send()
                one_of(half, 1, second_terms, second_got, second_sems, j, k).wait_send()
            side_of(half, j).wait_send()
    near.wait_send()
    for j in range(COT_CHUNKS):
        far(j).wait_send()
        relay(j).wait_send()
    for copy in (query_store, taps_store, key_store, value_store, weight_store):
        copy.wait()


def hand_over(*refs):
    sources, targets, held, sems = refs[:6], refs[6:12], refs[12:18], refs[18]
    loads = [pltpu.make_async_copy(a, b, sems.at[0, i]) for i, (a, b) in enumerate(zip(sources, held))]
    stores = [pltpu.make_async_copy(a, b, sems.at[1, i]) for i, (a, b) in enumerate(zip(held, targets))]
    for copy in loads:
        copy.start()
    for load, store in zip(loads, stores):
        load.wait()
        store.start()
    for copy in stores:
        copy.wait()


def body(query_gate, key_branch, value_branch, filter_taps, skip_gain, out_weight, out_grad):
    constants = [jnp.asarray(t) for t in tables()]
    blocks = (SEQ_BLOCKS, CHANS, 2 * COLS)
    bf16, f32 = jnp.bfloat16, jnp.float32
    in_hbm = pl.BlockSpec(memory_space=pl.ANY)
    in_vmem = pl.BlockSpec(memory_space=pltpu.VMEM)
    block_buffer = pltpu.VMEM(blocks, bf16)
    spec_buffer = pltpu.VMEM((CHANS * ROWS, 2 * COLS), f32)
    terms_buffer = pltpu.VMEM((2, 4, 256, 1024), bf16)
    second_buffer = pltpu.VMEM((2, 4, 256, 256), bf16)
    third_buffer = pltpu.VMEM((2, 256, LANES), bf16)
    dma = pltpu.SemaphoreType.DMA
    shapes = (
        jax.ShapeDtypeStruct(blocks, bf16),
        jax.ShapeDtypeStruct(blocks, bf16),
        jax.ShapeDtypeStruct(blocks, bf16),
        jax.ShapeDtypeStruct(filter_taps.shape, f32),
        jax.ShapeDtypeStruct((1, CHANS), f32),
        jax.ShapeDtypeStruct((512, LANES), f32),
    )
    results = pl.pallas_call(
        kernel,
        out_shape=shapes,
        in_specs=[in_hbm] * 4 + [in_vmem] + [in_hbm] * 6,
        out_specs=[in_hbm] * 4 + [in_vmem, in_hbm],
        scratch_shapes=[
            block_buffer, block_buffer, block_buffer,
            pltpu.VMEM(filter_taps.shape, f32),
            pltpu.VMEM(out_weight.shape, bf16),
            *[pltpu.VMEM(t.shape, f32) for t in constants],
            *[pltpu.VMEM(t.shape, bf16) for t in (constants[0], constants[1], constants[3])],
            pltpu.VMEM((4, 512, 1024), bf16),
            *[block_buffer] * 8,
            terms_buffer, terms_buffer, second_buffer, second_buffer, third_buffer, third_buffer,
            pltpu.VMEM((512, 512), f32),
            pltpu.VMEM((512, 512), bf16),
            pltpu.VMEM((2, CHANS * ROWS, LANES), f32),
            pltpu.VMEM((CHANS * ROWS, 2 * COLS), bf16),
            *[spec_buffer] * 4,
            block_buffer, block_buffer, block_buffer,
            pltpu.VMEM(filter_taps.shape, f32),
            pltpu.VMEM((512, LANES), f32),
            dma((10,)), dma((5,)),
            *[dma((2,))] * 4,
            dma((2, 2, TERM_CHUNKS, 3)), dma((2, 2, TERM_CHUNKS, 3)), dma((2, 2, TERM_CHUNKS)),
            dma((2,)), dma((2, COT_CHUNKS)), dma((2, COT_CHUNKS)),
        ],
        compiler_params=pltpu.CompilerParams(
            collective_id=0, has_side_effects=True, vmem_limit_bytes=56 * 1024 * 1024
        ),
    )(
        query_gate.reshape(blocks), key_branch.reshape(blocks), value_branch.reshape(blocks), filter_taps,
        skip_gain[None, :], out_weight, out_grad, *constants,
    )
    grad_query, grad_key, grad_value, grad_filter, grad_skip, grad_weight = pl.pallas_call(
        hand_over,
        out_shape=shapes,
        in_specs=[in_hbm] * 6,
        out_specs=[in_hbm] * 6,
        scratch_shapes=[*[pltpu.VMEM(t.shape, t.dtype) for t in shapes], dma((2, 6))],
        compiler_params=pltpu.CompilerParams(vmem_limit_bytes=56 * 1024 * 1024),
    )(*results)
    shape = query_gate.shape
    return (
        grad_query.reshape(shape), grad_key.reshape(shape), grad_value.reshape(shape),
        grad_filter, grad_skip[0], grad_weight,
    )


def solution(mesh):
    placed = (
        P("tp", "ctx"),
        P("tp", "ctx"),
        P("tp", "ctx"),
        P(("tp", "ctx"), None),
        P(("tp", "ctx")),
        P("tp", None),
        P("ctx", "tp"),
    )
    return jax.shard_map(
        body,
        mesh=mesh,
        in_specs=placed,
        out_specs=(
            P("tp", "ctx"),
            P("tp", "ctx"),
            P("tp", "ctx"),
            P(("tp", "ctx"), None),
            P(("tp", "ctx")),
            P("tp", "ctx"),
        ),
        check_vma=False,
    )
```

```python
import numpy as np
import ml_dtypes
import jax
import jax.numpy as jnp
from jax import lax
from jax.experimental import pallas as pl
from jax.experimental.pallas import tpu as pltpu
from jax.sharding import PartitionSpec as P

ROWS = 64
COLS = 256
LANES = 128
CHANS = 16
SEQ_BLOCKS = 32
TERM_CHUNKS = 2
Z_FIRST = 192
TERM_SPANS = ((0, Z_FIRST), (Z_FIRST, 512))


def bf16_pair(values):
    high = values.astype(ml_dtypes.bfloat16)
    low = (values - high.astype(np.float64)).astype(ml_dtypes.bfloat16)
    return high, low


def tables():
    ka = np.arange(ROWS) + 0.5
    phase_a = 2.0 * np.pi * np.outer(ka, np.arange(ROWS)) / (2 * ROWS)
    first = np.concatenate([np.cos(phase_a), -np.sin(phase_a)], axis=0)
    high, low = bf16_pair(first)
    first = np.concatenate([high, low, high], axis=1)
    last = np.concatenate([np.cos(phase_a).T, np.sin(phase_a).T], axis=1) / (ROWS * COLS)
    last = last.astype(ml_dtypes.bfloat16)
    last = np.concatenate([last, last], axis=1)
    phase_t = 2.0 * np.pi * np.outer(ka, np.arange(COLS)) / (2 * ROWS * COLS)
    turn = np.concatenate([np.cos(phase_t), np.sin(phase_t)], axis=1).astype(np.float32)
    phase_b = 2.0 * np.pi * (np.outer(np.arange(COLS), np.arange(COLS)) % COLS) / COLS
    cos_b, sin_b = np.cos(phase_b), np.sin(phase_b)
    second = np.block([[cos_b, -sin_b], [sin_b, cos_b]]).astype(ml_dtypes.bfloat16)
    return [t.astype(np.float32) for t in (first, last, turn, second)]


def dot(left, right):
    return jnp.dot(left, right, preferred_element_type=jnp.float32)


def turned(re, im, turn_ref):
    cos, sin = turn_ref[:, :COLS], turn_ref[:, COLS:]
    return re * cos + im * sin, im * cos - re * sin


def take_blocks(blocks_ref, grid):
    def step(s, carry):
        block = blocks_ref[s].astype(jnp.float32)
        for part in range(4):
            rows = pl.ds(pl.multiple_of(s * 32 + part // 2 * CHANS, CHANS), CHANS)
            grid[part % 2, rows, :] = block[:, part * LANES : (part + 1) * LANES]
        return carry

    lax.fori_loop(0, SEQ_BLOCKS, step, 0, unroll=4)


def second_stage(mixed, second_ref, out):
    out[...] = dot(mixed[...], second_ref[...])


def spectrum_of(grid, first_ref, turn_ref, second_ref, mixed, out, wide):
    def step(c, carry):
        rows = pl.ds(c, ROWS, stride=CHANS)
        signal = jnp.concatenate([grid[0, rows, :], grid[1, rows, :]], axis=1)
        high = signal.astype(jnp.bfloat16)
        if wide:
            low = (signal - high.astype(jnp.float32)).astype(jnp.bfloat16)
            left, right = first_ref[...], jnp.concatenate([high, high, low], axis=0)
        else:
            left, right = first_ref[:, : 2 * ROWS], jnp.concatenate([high, high], axis=0)
        part = dot(left, right)
        re, im = turned(part[:ROWS], part[ROWS:], turn_ref)
        rows = pl.ds(pl.multiple_of(c * ROWS, ROWS), ROWS)
        mixed[rows, :COLS] = re.astype(jnp.bfloat16)
        mixed[rows, COLS:] = im.astype(jnp.bfloat16)
        return carry

    lax.fori_loop(0, CHANS, step, 0, unroll=16)
    second_stage(mixed, second_ref, out)


def product_to(mixed, left, right, conj):
    def step(i, carry):
        rows = pl.ds(pl.multiple_of(i * ROWS, ROWS), ROWS)
        lr, li = left[rows, :COLS], left[rows, COLS:]
        rr, ri = right[rows, :COLS], right[rows, COLS:]
        if conj:
            re, im = lr * rr + li * ri, li * rr - lr * ri
        else:
            re, im = lr * rr - li * ri, -(lr * ri + li * rr)
        mixed[rows, :COLS] = re.astype(jnp.bfloat16)
        mixed[rows, COLS:] = im.astype(jnp.bfloat16)
        return carry

    lax.fori_loop(0, CHANS, step, 0, unroll=2)


def signal_of(mixed, last_ref, turn_ref, second_ref, spec, grid):
    second_stage(mixed, second_ref, spec)

    def step(c, carry):
        rows = pl.ds(pl.multiple_of(c * ROWS, ROWS), ROWS)
        re, im = turned(spec[rows, :COLS], spec[rows, COLS:], turn_ref)
        both = jnp.concatenate([re, im], axis=0)
        high = both.astype(jnp.bfloat16)
        low = (both - high.astype(jnp.float32)).astype(jnp.bfloat16)
        signal = dot(last_ref[...], jnp.concatenate([high, low], axis=0))
        for half in range(2):
            grid[half, pl.ds(c, ROWS, stride=CHANS), :] = signal[:, half * LANES : (half + 1) * LANES]
        return carry

    lax.fori_loop(0, CHANS, step, 0, unroll=16)


def give_blocks(grid, blocks_ref):
    def step(s, carry):
        for part in range(4):
            rows = pl.ds(pl.multiple_of(s * 32 + part // 2 * CHANS, CHANS), CHANS)
            blocks_ref[s, :, part * LANES : (part + 1) * LANES] = grid[part % 2, rows, :].astype(jnp.bfloat16)
        return carry

    lax.fori_loop(0, SEQ_BLOCKS, step, 0, unroll=4)


def taps_to_grid(taps, skip_ref, grid):
    for a in range(ROWS):
        for half in range(2):
            start = a * COLS + half * LANES
            grid[half, a * CHANS : (a + 1) * CHANS, :] = taps[:, start : start + LANES]
    row = lax.broadcasted_iota(jnp.int32, (CHANS, CHANS), 0)
    col = lax.broadcasted_iota(jnp.int32, (CHANS, CHANS), 1)
    skip = jnp.sum(jnp.where(row == col, skip_ref[...], 0.0), axis=1, keepdims=True)
    lane = lax.broadcasted_iota(jnp.int32, (CHANS, LANES), 1)
    grid[0, :CHANS, :] += jnp.where(lane == 0, skip, 0.0)


def grid_to_taps(grid, taps):
    for a in range(ROWS):
        for half in range(2):
            start = a * COLS + half * LANES
            taps[:, start : start + LANES] = grid[half, a * CHANS : (a + 1) * CHANS, :]


def skip_gradient(grad, gated, out_ref):
    def step(s, total):
        return total + grad[s].astype(jnp.float32) * gated[s].astype(jnp.float32)

    total = lax.fori_loop(0, SEQ_BLOCKS, step, jnp.zeros((CHANS, 2 * COLS), jnp.float32))
    total = jnp.sum(total, axis=1, keepdims=True)
    row = lax.broadcasted_iota(jnp.int32, (CHANS, CHANS), 0)
    col = lax.broadcasted_iota(jnp.int32, (CHANS, CHANS), 1)
    out_ref[...] = jnp.sum(jnp.where(row == col, total, 0.0), axis=0, keepdims=True)


def for_blocks(step, unroll=4):
    def body(s, carry):
        step(s)
        return carry

    lax.fori_loop(0, SEQ_BLOCKS, body, 0, unroll=unroll)


def block_rows(s):
    return pl.ds(pl.multiple_of(s * CHANS, CHANS), CHANS)


def kernel(
    query_in, key_in, value_in, taps_in, skip_ref, weight_in, cot_in, first_in, last_in, turn_in, second_in,
    query_out, key_out, value_out, taps_out, skip_out, weight_out,
    query, key, value, taps, weight, first_wide, last_wide, turn, second_wide, first, last, second,
    cot, gated, gated_got, conv, conv_got, grad, grad_got, back, back_got,
    terms_z, terms_y, terms_got_z, terms_got_y, second_z, second_y, second_got_z, second_got_y,
    third_z, third_y, third_got_z, third_got_y, grad_mixed, gate_mixed,
    grid, mixed, spec, taps_spec, gated_spec, grad_spec, query_res, key_res, value_res, taps_res, weight_res,
    load_sem, store_sem, gated_sems, conv_sems, grad_sems, back_sems, terms_sems, second_sems, third_sems,
    near_sems, far_sems, relay_sems,
):
    terms, terms_got = (terms_z, terms_y), (terms_got_z, terms_got_y)
    second_terms, second_got = (second_z, second_y), (second_got_z, second_got_y)
    third, third_got = (third_z, third_y), (third_got_z, third_got_y)
    me = lax.axis_index("ctx")
    part = lax.axis_index("tp")
    sibling = part + 1 - 2 * (part % 2)
    across = (part + 2) % 4
    diagonal = (sibling + 2) % 4

    def load(index, source, target):
        copy = pltpu.make_async_copy(source, target, load_sem.at[index])
        copy.start()
        return copy

    key_load = load(0, key_in, key)
    value_load = load(1, value_in, value)
    cot_load = load(2, cot_in, cot.at[part])
    first_load = load(3, first_in, first_wide)
    turn_load = load(4, turn_in, turn)
    second_load = load(5, second_in, second_wide)
    taps_load = load(6, taps_in, taps)
    last_load = load(7, last_in, last_wide)
    weight_load = load(8, weight_in, weight)
    query_load = load(9, query_in, query)

    barrier = pltpu.get_barrier_semaphore()

    def greet(i, carry):
        pl.semaphore_signal(
            barrier, inc=1, device_id={"ctx": (me + i) % SEQ_BLOCKS}, device_id_type=pl.DeviceIdType.MESH
        )
        return carry

    lax.fori_loop(1, SEQ_BLOCKS, greet, 0)
    for other in (sibling, across):
        pl.semaphore_signal(barrier, inc=1, device_id={"tp": other}, device_id_type=pl.DeviceIdType.MESH)

    key_load.wait()
    value_load.wait()

    def gate(s):
        gated[s] = (key[s].astype(jnp.float32) * value[s].astype(jnp.float32)).astype(jnp.bfloat16)

    for_blocks(gate)
    pl.semaphore_wait(barrier, SEQ_BLOCKS + 1)

    def to_device(source, target, send_sem, recv_sem, device):
        return pltpu.make_async_remote_copy(
            src_ref=source,
            dst_ref=target,
            send_sem=send_sem,
            recv_sem=recv_sem,
            device_id=device,
            device_id_type=pl.DeviceIdType.MESH,
        )

    def exchange(source, target, sems):
        def step(i, carry):
            peer = (me + i) % SEQ_BLOCKS
            to_device(source.at[peer], target.at[me], sems.at[0], sems.at[1], {"ctx": peer}).start()
            return carry

        lax.fori_loop(1, SEQ_BLOCKS, step, 0)
        target[me] = source[me]

    def whole_exchange(source, target, sems):
        blocks = pl.ds(0, SEQ_BLOCKS - 1)
        return to_device(source.at[blocks], target.at[blocks], sems.at[0], sems.at[1], {"tp": across})

    def arrived(source, target, sems):
        whole_exchange(source, target, sems).wait_recv()

    def sent(source, target, sems):
        whole_exchange(source, target, sems).wait_send()

    exchange(gated, gated_got, gated_sems)

    near = pltpu.make_async_remote_copy(
        src_ref=cot_in,
        dst_ref=cot.at[part],
        send_sem=near_sems.at[0],
        recv_sem=near_sems.at[1],
        device_id={"tp": sibling},
        device_id_type=pl.DeviceIdType.MESH,
    )
    near.start()

    def cot_block(p, parity, half, q):
        columns = pl.ds(q * 256 + parity * LANES, LANES)
        return cot.at[p, pl.ds(half * 256, 256), columns]

    def chunk_bytes(p, parity, half, sems, device):
        window = cot.at[p, pl.ds(half * 256, 256), pl.ds(0, 512)]
        return to_device(window, window, sems.at[0, parity, half], sems.at[1, parity, half], device)

    def far_start(parity, half):
        for q in range(4):
            columns = pl.ds(q * 256 + parity * LANES, LANES)
            to_device(
                cot_in.at[pl.ds(half * 256, 256), columns], cot_block(part, parity, half, q),
                far_sems.at[0, parity, half], far_sems.at[1, parity, half], {"tp": across},
            ).start()

    def relay_start(parity, half):
        chunk_bytes(across, parity, half, far_sems, {"tp": across}).wait_recv()
        for q in range(4):
            block = cot_block(across, parity, half, q)
            to_device(
                block, block, relay_sems.at[0, parity, half], relay_sems.at[1, parity, half], {"tp": sibling}
            ).start()

    def relay_arrived(parity, half):
        chunk_bytes(diagonal, parity, half, relay_sems, {"tp": sibling}).wait_recv()

    taps_load.wait()
    first_load.wait()
    turn_load.wait()
    second_load.wait()
    first[...] = first_wide[...].astype(jnp.bfloat16)
    second[...] = second_wide[...].astype(jnp.bfloat16)
    taps_to_grid(taps, skip_ref, grid)
    spectrum_of(grid, first, turn, second, mixed, taps_spec, True)

    def mix_features(p, fresh, halves=(0, 1)):
        columns = pl.ds(pl.multiple_of(p * 1024, 1024), 1024)
        for half in halves:
            rows = pl.ds(half * 256, 256)
            term = lax.dot_general(
                weight[:, columns], cot[p, rows, :], (((1,), (1,)), ((), ())),
                preferred_element_type=jnp.float32,
            )
            if fresh:
                grad_mixed[:, rows] = term
            else:
                grad_mixed[:, rows] += term

    def mix_chunk(p, parity, half):
        rows = pl.ds(half * 256, 256)
        left = [
            weight[:, pl.ds(pl.multiple_of(p * 1024 + q * 256 + parity * LANES, LANES), LANES)] for q in range(4)
        ]
        right = [cot[p, rows, pl.ds(q * 256 + parity * LANES, LANES)] for q in range(4)]
        grad_mixed[:, rows] += lax.dot_general(
            jnp.concatenate(left, axis=1), jnp.concatenate(right, axis=1), (((1,), (1,)), ((), ())),
            preferred_element_type=jnp.float32,
        )

    cot_load.wait()
    weight_load.wait()
    mix_features(part, True)
    last_load.wait()
    last[...] = last_wide[...].astype(jnp.bfloat16)
    query_load.wait()

    arrived(gated, gated_got, gated_sems)
    far_start(0, 0)
    take_blocks(gated_got, grid)
    spectrum_of(grid, first, turn, second, mixed, gated_spec, False)
    product_to(mixed, taps_spec, gated_spec, False)
    signal_of(mixed, last, turn, second, spec, grid)
    give_blocks(grid, conv)
    exchange(conv, conv_got, conv_sems)

    def half_exchange(half, source, target, peer):
        columns = pl.ds(half * 256, 256)
        return to_device(
            source.at[peer, :, columns], target.at[me, :, columns], grad_sems.at[0, half], grad_sems.at[1, half],
            {"ctx": peer},
        )

    def whole_half(half):
        blocks, columns = pl.ds(0, SEQ_BLOCKS - 1), pl.ds(half * 256, 256)
        return to_device(
            grad.at[blocks, :, columns], grad_got.at[blocks, :, columns], grad_sems.at[0, half],
            grad_sems.at[1, half], {"tp": across},
        )

    def take_chunk(parity, half):
        relay_start(parity, half)
        mix_chunk(across, parity, half)
        relay_arrived(parity, half)
        mix_chunk(diagonal, parity, half)

    def send_gradient(half):
        columns = pl.ds(half * 256, 256)

        def cotangent(s):
            grad[s, :, columns] = (
                grad_mixed[block_rows(s), columns] * query[s, :, columns].astype(jnp.float32)
            ).astype(jnp.bfloat16)

        for_blocks(cotangent)

        def step(i, carry):
            half_exchange(half, grad, grad_got, (me + i) % SEQ_BLOCKS).start()
            return carry

        lax.fori_loop(1, SEQ_BLOCKS, step, 0)
        grad_got[me, :, columns] = grad[me, :, columns]

    near.wait_recv()
    mix_features(sibling, False)
    arrived(conv, conv_got, conv_sems)
    far_start(0, 1)
    far_start(1, 0)
    far_start(1, 1)

    def gate_output(s):
        gate_mixed[block_rows(s), :] = (
            query[s].astype(jnp.float32) * conv_got[s].astype(jnp.float32)
        ).astype(jnp.bfloat16)

    for_blocks(gate_output)

    z, y, x = me // 8, me // 2 % 4, me % 2
    chip = part // 2

    def peer_of(order, stage, k):
        if order == stage:
            return (z + k) % 4, {"ctx": (z + k) % 4 * 8 + y * 2 + x}, z
        return (y + k) % 4, {"ctx": z * 8 + (y + k) % 4 * 2 + x}, y

    def chunk_span(order, j):
        start, stop = TERM_SPANS[order]
        rows = (stop - start) // TERM_CHUNKS
        return pl.ds(j * rows, rows)

    def first_columns(order, piece):
        if order == 0:
            return pl.ds(0, 1024) if piece == 0 else pl.ds((piece - 1) * 512, 512)
        if piece == 0:
            return pl.ds(pl.multiple_of(chip * 512, 512), 512)
        return pl.ds(pl.multiple_of((1 - chip) * 512 + (piece - 1) * 256, 256), 256)

    def first_send(order, piece, j, k):
        place, device, own = peer_of(order, 0, k)
        rows, columns = chunk_span(order, j), first_columns(order, piece)
        return to_device(
            terms[order].at[place, rows, columns], terms_got[order].at[own, rows, columns],
            terms_sems.at[0, order, j, k - 1], terms_sems.at[1, order, j, k - 1], device,
        )

    def first_whole(order, j, k):
        place, device, own = peer_of(order, 0, 4 - k)
        rows = chunk_span(order, j)
        return to_device(
            terms[order].at[place, rows], terms_got[order].at[place, rows],
            terms_sems.at[0, order, j, k - 1], terms_sems.at[1, order, j, k - 1], device,
        )

    def second_send(order, j, k):
        place, device, own = peer_of(order, 1, k)
        rows = chunk_span(order, j)
        return to_device(
            second_terms[order].at[place, rows], second_got[order].at[own, rows],
            second_sems.at[0, order, j, k - 1], second_sems.at[1, order, j, k - 1], device,
        )

    def second_arrival(order, j, k):
        place, device, own = peer_of(order, 1, 4 - k)
        rows = chunk_span(order, j)
        return to_device(
            second_terms[order].at[place, rows], second_got[order].at[place, rows],
            second_sems.at[0, order, j, k - 1], second_sems.at[1, order, j, k - 1], device,
        )

    def side_of(order, j):
        rows = chunk_span(order, j)
        return to_device(
            third[order].at[rows], third_got[order].at[rows],
            third_sems.at[0, order, j], third_sems.at[1, order, j], {"ctx": me + 1 - 2 * x},
        )

    def keep_term(p, q, parity, term):
        columns = pl.ds(pl.multiple_of(parity * 512 + q * LANES, LANES), LANES)
        terms[0][p, :, columns] = term[:Z_FIRST]
        columns = pl.ds(pl.multiple_of(p // 2 * 512 + parity * 256 + p % 2 * LANES, LANES), LANES)
        terms[1][q, :, columns] = term[Z_FIRST:]

    def make_terms():
        def step(i, carry):
            p, q = chip * 2 + i // 4, i % 4
            columns = pl.ds(pl.multiple_of(q * 256, 256), 256)
            term = dot(gate_mixed[...], cot[p, :, columns]).astype(jnp.bfloat16)
            for parity in range(2):
                keep_term(p, q, parity, term[:, parity * LANES : (parity + 1) * LANES])
            return carry

        lax.fori_loop(0, 8, step, 0)

    def make_late_terms(parity):
        def step(i, carry):
            p, q = (1 - chip) * 2 + i // 2, i % 2 * 2
            right = [
                cot[p, :, pl.ds(pl.multiple_of((q + n) * 256 + parity * LANES, LANES), LANES)] for n in range(2)
            ]
            term = dot(gate_mixed[...], jnp.concatenate(right, axis=1)).astype(jnp.bfloat16)
            for n in range(2):
                keep_term(p, q + n, parity, term[:, n * LANES : (n + 1) * LANES])
            return carry

        lax.fori_loop(0, 4, step, 0)

    def send_terms(piece):
        for j in range(TERM_CHUNKS):
            for k in (2, 1, 3):
                first_send(1, piece, j, k).start()
                here = (z + k) % 4 // 2 == chip

                @pl.when(here if piece == 0 else jnp.logical_not(here))
                def _():
                    first_send(0, piece, j, k).start()

    make_terms()
    send_terms(0)
    take_chunk(0, 0)
    take_chunk(0, 1)
    make_late_terms(0)
    send_terms(1)
    take_chunk(1, 0)
    send_gradient(0)
    take_chunk(1, 1)
    send_gradient(1)
    make_late_terms(1)
    send_terms(2)

    def query_gradient(s):
        query_res[s] = (grad_mixed[block_rows(s), :] * conv_got[s].astype(jnp.float32)).astype(jnp.bfloat16)

    for_blocks(query_gradient)
    query_store = pltpu.make_async_copy(query_res, query_out, store_sem.at[0])
    query_store.start()

    for half in range(2):
        whole_half(half).wait_recv()
    take_blocks(grad_got, grid)
    spectrum_of(grid, first, turn, second, mixed, grad_spec, False)
    product_to(mixed, taps_spec, grad_spec, True)
    signal_of(mixed, last, turn, second, spec, grid)
    give_blocks(grid, back)
    exchange(back, back_got, back_sems)
    product_to(mixed, gated_spec, grad_spec, True)
    signal_of(mixed, last, turn, second, spec, grid)
    grid_to_taps(grid, taps_res)
    taps_store = pltpu.make_async_copy(taps_res, taps_out, store_sem.at[1])
    taps_store.start()
    skip_gradient(grad_got, gated_got, skip_out)

    def summed(order, stage, held, got, j, columns):
        own = z if order == stage else y
        rows = chunk_span(order, j)
        total = held[order][own, rows, columns].astype(jnp.float32)
        for k in (1, 2, 3):
            total += got[order][(own + k) % 4, rows, columns].astype(jnp.float32)
        return total

    for j in range(TERM_CHUNKS):
        for order in range(2):
            for k in (1, 3, 2):
                first_whole(order, j, k).wait_recv()
            for place in range(4):
                for parity in range(2):
                    if order == 0:
                        start = parity * 512 + place * LANES
                    else:
                        start = place // 2 * 512 + parity * 256 + place % 2 * LANES
                    total = summed(order, 0, terms, terms_got, j, pl.ds(start, LANES))
                    columns = pl.ds(parity * LANES, LANES)
                    second_terms[order][place, chunk_span(order, j), columns] = total.astype(jnp.bfloat16)
            for k in (2, 1, 3):
                second_send(order, j, k).start()

    arrived(back, back_got, back_sems)

    def gate_input(s):
        back_f = back_got[s].astype(jnp.float32)
        key_res[s] = (back_f * value[s].astype(jnp.float32)).astype(jnp.bfloat16)
        value_res[s] = (back_f * key[s].astype(jnp.float32)).astype(jnp.bfloat16)

    for_blocks(gate_input)
    key_store = pltpu.make_async_copy(key_res, key_out, store_sem.at[2])
    key_store.start()
    value_store = pltpu.make_async_copy(value_res, value_out, store_sem.at[3])
    value_store.start()
    mine = pl.ds(pl.multiple_of(x * LANES, LANES), LANES)
    others = pl.ds(pl.multiple_of((1 - x) * LANES, LANES), LANES)

    def result_rows(order, j):
        start, stop = TERM_SPANS[order]
        rows = (stop - start) // TERM_CHUNKS
        return pl.ds(start + j * rows, rows)

    for j in range(TERM_CHUNKS):
        for order in range(2):
            for k in (1, 3, 2):
                second_arrival(order, j, k).wait_recv()
            total = summed(order, 1, second_terms, second_got, j, others)
            third[order][chunk_span(order, j)] = total.astype(jnp.bfloat16)
            side_of(order, j).start()
            weight_res[result_rows(order, j), :] = summed(order, 1, second_terms, second_got, j, mine)
    for j in range(TERM_CHUNKS):
        for order in range(2):
            side_of(order, j).wait_recv()
            weight_res[result_rows(order, j), :] += third_got[order][chunk_span(order, j)].astype(jnp.float32)
    weight_store = pltpu.make_async_copy(weight_res, weight_out, store_sem.at[4])
    weight_store.start()

    sent(gated, gated_got, gated_sems)
    sent(conv, conv_got, conv_sems)
    for half in range(2):
        whole_half(half).wait_send()
    sent(back, back_got, back_sems)
    for j in range(TERM_CHUNKS):
        for order in range(2):
            for k in (1, 2, 3):
                first_whole(order, j, k).wait_send()
                second_send(order, j, k).wait_send()
            side_of(order, j).wait_send()
    near.wait_send()
    for parity in range(2):
        for half in range(2):
            chunk_bytes(part, parity, half, far_sems, {"tp": across}).wait_send()
            chunk_bytes(across, parity, half, relay_sems, {"tp": sibling}).wait_send()
    for copy in (query_store, taps_store, key_store, value_store, weight_store):
        copy.wait()


def hand_over(*refs):
    sources, targets, held, sems = refs[:6], refs[6:12], refs[12:18], refs[18]
    loads = [pltpu.make_async_copy(a, b, sems.at[0, i]) for i, (a, b) in enumerate(zip(sources, held))]
    stores = [pltpu.make_async_copy(a, b, sems.at[1, i]) for i, (a, b) in enumerate(zip(held, targets))]
    for copy in loads:
        copy.start()
    for load, store in zip(loads, stores):
        load.wait()
        store.start()
    for copy in stores:
        copy.wait()


def body(query_gate, key_branch, value_branch, filter_taps, skip_gain, out_weight, out_grad):
    constants = [jnp.asarray(t) for t in tables()]
    blocks = (SEQ_BLOCKS, CHANS, 2 * COLS)
    bf16, f32 = jnp.bfloat16, jnp.float32
    in_hbm = pl.BlockSpec(memory_space=pl.ANY)
    in_vmem = pl.BlockSpec(memory_space=pltpu.VMEM)
    block_buffer = pltpu.VMEM(blocks, bf16)
    spec_buffer = pltpu.VMEM((CHANS * ROWS, 2 * COLS), f32)
    spans = [stop - start for start, stop in TERM_SPANS]
    terms_buffers = [pltpu.VMEM((4, rows, 1024), bf16) for rows in spans]
    second_buffers = [pltpu.VMEM((4, rows, 256), bf16) for rows in spans]
    third_buffers = [pltpu.VMEM((rows, LANES), bf16) for rows in spans]
    dma = pltpu.SemaphoreType.DMA
    shapes = (
        jax.ShapeDtypeStruct(blocks, bf16),
        jax.ShapeDtypeStruct(blocks, bf16),
        jax.ShapeDtypeStruct(blocks, bf16),
        jax.ShapeDtypeStruct(filter_taps.shape, f32),
        jax.ShapeDtypeStruct((1, CHANS), f32),
        jax.ShapeDtypeStruct((512, LANES), f32),
    )
    results = pl.pallas_call(
        kernel,
        out_shape=shapes,
        in_specs=[in_hbm] * 4 + [in_vmem] + [in_hbm] * 6,
        out_specs=[in_hbm] * 4 + [in_vmem, in_hbm],
        scratch_shapes=[
            block_buffer, block_buffer, block_buffer,
            pltpu.VMEM(filter_taps.shape, f32),
            pltpu.VMEM(out_weight.shape, bf16),
            *[pltpu.VMEM(t.shape, f32) for t in constants],
            *[pltpu.VMEM(t.shape, bf16) for t in (constants[0], constants[1], constants[3])],
            pltpu.VMEM((4, 512, 1024), bf16),
            *[block_buffer] * 8,
            *terms_buffers * 2, *second_buffers * 2, *third_buffers * 2,
            pltpu.VMEM((512, 512), f32),
            pltpu.VMEM((512, 512), bf16),
            pltpu.VMEM((2, CHANS * ROWS, LANES), f32),
            pltpu.VMEM((CHANS * ROWS, 2 * COLS), bf16),
            *[spec_buffer] * 4,
            block_buffer, block_buffer, block_buffer,
            pltpu.VMEM(filter_taps.shape, f32),
            pltpu.VMEM((512, LANES), f32),
            dma((10,)), dma((5,)),
            dma((2,)), dma((2,)), dma((2, 2)), dma((2,)),
            dma((2, 2, TERM_CHUNKS, 3)), dma((2, 2, TERM_CHUNKS, 3)), dma((2, 2, TERM_CHUNKS)),
            dma((2,)), dma((2, 2, 2)), dma((2, 2, 2)),
        ],
        compiler_params=pltpu.CompilerParams(
            collective_id=0, has_side_effects=True, vmem_limit_bytes=56 * 1024 * 1024
        ),
    )(
        query_gate.reshape(blocks), key_branch.reshape(blocks), value_branch.reshape(blocks), filter_taps,
        skip_gain[None, :], out_weight, out_grad, *constants,
    )
    grad_query, grad_key, grad_value, grad_filter, grad_skip, grad_weight = pl.pallas_call(
        hand_over,
        out_shape=shapes,
        in_specs=[in_hbm] * 6,
        out_specs=[in_hbm] * 6,
        scratch_shapes=[*[pltpu.VMEM(t.shape, t.dtype) for t in shapes], dma((2, 6))],
        compiler_params=pltpu.CompilerParams(vmem_limit_bytes=56 * 1024 * 1024),
    )(*results)
    shape = query_gate.shape
    return (
        grad_query.reshape(shape), grad_key.reshape(shape), grad_value.reshape(shape),
        grad_filter, grad_skip[0], grad_weight,
    )


def solution(mesh):
    placed = (
        P("tp", "ctx"),
        P("tp", "ctx"),
        P("tp", "ctx"),
        P(("tp", "ctx"), None),
        P(("tp", "ctx")),
        P("tp", None),
        P("ctx", "tp"),
    )
    return jax.shard_map(
        body,
        mesh=mesh,
        in_specs=placed,
        out_specs=(
            P("tp", "ctx"),
            P("tp", "ctx"),
            P("tp", "ctx"),
            P(("tp", "ctx"), None),
            P(("tp", "ctx")),
            P("tp", "ctx"),
        ),
        check_vma=False,
    )
```

```python
import numpy as np
import ml_dtypes
import jax
import jax.numpy as jnp
from jax import lax
from jax.experimental import pallas as pl
from jax.experimental.pallas import tpu as pltpu
from jax.sharding import PartitionSpec as P

ROWS = 64
COLS = 256
LANES = 128
CHANS = 16
SEQ_BLOCKS = 32
Z_FIRST = 192
TERM_SPANS = ((0, Z_FIRST), (Z_FIRST, 512))


def bf16_pair(values):
    high = values.astype(ml_dtypes.bfloat16)
    low = (values - high.astype(np.float64)).astype(ml_dtypes.bfloat16)
    return high, low


def tables():
    ka = np.arange(ROWS) + 0.5
    phase_a = 2.0 * np.pi * np.outer(ka, np.arange(ROWS)) / (2 * ROWS)
    first = np.concatenate([np.cos(phase_a), -np.sin(phase_a)], axis=0)
    high, low = bf16_pair(first)
    first = np.concatenate([high, low, high], axis=1)
    last = np.concatenate([np.cos(phase_a).T, np.sin(phase_a).T], axis=1) / (ROWS * COLS)
    last = last.astype(ml_dtypes.bfloat16)
    last = np.concatenate([last, last], axis=1)
    phase_t = 2.0 * np.pi * np.outer(ka, np.arange(COLS)) / (2 * ROWS * COLS)
    turn = np.concatenate([np.cos(phase_t), np.sin(phase_t)], axis=1).astype(np.float32)
    phase_b = 2.0 * np.pi * (np.outer(np.arange(COLS), np.arange(COLS)) % COLS) / COLS
    cos_b, sin_b = np.cos(phase_b), np.sin(phase_b)
    second = np.block([[cos_b, -sin_b], [sin_b, cos_b]]).astype(ml_dtypes.bfloat16)
    return [t.astype(np.float32) for t in (first, last, turn, second)]


def dot(left, right):
    return jnp.dot(left, right, preferred_element_type=jnp.float32)


def turned(re, im, turn_ref):
    cos, sin = turn_ref[:, :COLS], turn_ref[:, COLS:]
    return re * cos + im * sin, im * cos - re * sin


def take_blocks(blocks_ref, grid):
    def step(s, carry):
        block = blocks_ref[s].astype(jnp.float32)
        for part in range(4):
            rows = pl.ds(pl.multiple_of(s * 32 + part // 2 * CHANS, CHANS), CHANS)
            grid[part % 2, rows, :] = block[:, part * LANES : (part + 1) * LANES]
        return carry

    lax.fori_loop(0, SEQ_BLOCKS, step, 0, unroll=4)


def second_stage(mixed, second_ref, out):
    out[...] = dot(mixed[...], second_ref[...])


def spectrum_of(grid, first_ref, turn_ref, second_ref, mixed, out, wide):
    def step(c, carry):
        rows = pl.ds(c, ROWS, stride=CHANS)
        signal = jnp.concatenate([grid[0, rows, :], grid[1, rows, :]], axis=1)
        high = signal.astype(jnp.bfloat16)
        if wide:
            low = (signal - high.astype(jnp.float32)).astype(jnp.bfloat16)
            left, right = first_ref[...], jnp.concatenate([high, high, low], axis=0)
        else:
            left, right = first_ref[:, : 2 * ROWS], jnp.concatenate([high, high], axis=0)
        part = dot(left, right)
        re, im = turned(part[:ROWS], part[ROWS:], turn_ref)
        rows = pl.ds(pl.multiple_of(c * ROWS, ROWS), ROWS)
        mixed[rows, :COLS] = re.astype(jnp.bfloat16)
        mixed[rows, COLS:] = im.astype(jnp.bfloat16)
        return carry

    lax.fori_loop(0, CHANS, step, 0, unroll=16)
    second_stage(mixed, second_ref, out)


def product_to(mixed, left, right, conj):
    def step(i, carry):
        rows = pl.ds(pl.multiple_of(i * ROWS, ROWS), ROWS)
        lr, li = left[rows, :COLS], left[rows, COLS:]
        rr, ri = right[rows, :COLS], right[rows, COLS:]
        if conj:
            re, im = lr * rr + li * ri, li * rr - lr * ri
        else:
            re, im = lr * rr - li * ri, -(lr * ri + li * rr)
        mixed[rows, :COLS] = re.astype(jnp.bfloat16)
        mixed[rows, COLS:] = im.astype(jnp.bfloat16)
        return carry

    lax.fori_loop(0, CHANS, step, 0, unroll=2)


def signal_of(mixed, last_ref, turn_ref, second_ref, spec, grid):
    second_stage(mixed, second_ref, spec)

    def step(c, carry):
        rows = pl.ds(pl.multiple_of(c * ROWS, ROWS), ROWS)
        re, im = turned(spec[rows, :COLS], spec[rows, COLS:], turn_ref)
        both = jnp.concatenate([re, im], axis=0)
        high = both.astype(jnp.bfloat16)
        low = (both - high.astype(jnp.float32)).astype(jnp.bfloat16)
        signal = dot(last_ref[...], jnp.concatenate([high, low], axis=0))
        for half in range(2):
            grid[half, pl.ds(c, ROWS, stride=CHANS), :] = signal[:, half * LANES : (half + 1) * LANES]
        return carry

    lax.fori_loop(0, CHANS, step, 0, unroll=16)


def give_blocks(grid, blocks_ref):
    def step(s, carry):
        for part in range(4):
            rows = pl.ds(pl.multiple_of(s * 32 + part // 2 * CHANS, CHANS), CHANS)
            blocks_ref[s, :, part * LANES : (part + 1) * LANES] = grid[part % 2, rows, :].astype(jnp.bfloat16)
        return carry

    lax.fori_loop(0, SEQ_BLOCKS, step, 0, unroll=4)


def taps_to_grid(taps, skip_ref, grid):
    for a in range(ROWS):
        for half in range(2):
            start = a * COLS + half * LANES
            grid[half, a * CHANS : (a + 1) * CHANS, :] = taps[:, start : start + LANES]
    row = lax.broadcasted_iota(jnp.int32, (CHANS, CHANS), 0)
    col = lax.broadcasted_iota(jnp.int32, (CHANS, CHANS), 1)
    skip = jnp.sum(jnp.where(row == col, skip_ref[...], 0.0), axis=1, keepdims=True)
    lane = lax.broadcasted_iota(jnp.int32, (CHANS, LANES), 1)
    grid[0, :CHANS, :] += jnp.where(lane == 0, skip, 0.0)


def grid_to_taps(grid, taps):
    for a in range(ROWS):
        for half in range(2):
            start = a * COLS + half * LANES
            taps[:, start : start + LANES] = grid[half, a * CHANS : (a + 1) * CHANS, :]


def skip_gradient(grad, gated, out_ref):
    def step(s, total):
        return total + grad[s].astype(jnp.float32) * gated[s].astype(jnp.float32)

    total = lax.fori_loop(0, SEQ_BLOCKS, step, jnp.zeros((CHANS, 2 * COLS), jnp.float32))
    total = jnp.sum(total, axis=1, keepdims=True)
    row = lax.broadcasted_iota(jnp.int32, (CHANS, CHANS), 0)
    col = lax.broadcasted_iota(jnp.int32, (CHANS, CHANS), 1)
    out_ref[...] = jnp.sum(jnp.where(row == col, total, 0.0), axis=0, keepdims=True)


def for_blocks(step, unroll=4):
    def body(s, carry):
        step(s)
        return carry

    lax.fori_loop(0, SEQ_BLOCKS, body, 0, unroll=unroll)


def block_rows(s):
    return pl.ds(pl.multiple_of(s * CHANS, CHANS), CHANS)


def kernel(
    query_in, key_in, value_in, taps_in, skip_ref, weight_in, cot_in, first_in, last_in, turn_in, second_in,
    query_res, key_res, value_res, taps_res, skip_out, weight_res,
    query, key, value, taps, weight, first_wide, last_wide, turn, second_wide, first, last, second,
    cot, gated, gated_got, conv, conv_got, grad, grad_got, back, back_got,
    terms_z, terms_y, terms_got_z, terms_got_y, second_z, second_y, second_got_z, second_got_y,
    third_z, third_y, third_got_z, third_got_y, grad_mixed, gate_mixed,
    grid, mixed, spec, taps_spec, gated_spec, grad_spec,
    load_sem, gated_sems, conv_sems, grad_sems, back_sems, terms_sems, second_sems, third_sems,
    near_sems, far_sems, relay_sems,
):
    terms, terms_got = (terms_z, terms_y), (terms_got_z, terms_got_y)
    second_terms, second_got = (second_z, second_y), (second_got_z, second_got_y)
    third, third_got = (third_z, third_y), (third_got_z, third_got_y)
    me = lax.axis_index("ctx")
    part = lax.axis_index("tp")
    sibling = part + 1 - 2 * (part % 2)
    across = (part + 2) % 4
    diagonal = (sibling + 2) % 4

    def load(index, source, target):
        copy = pltpu.make_async_copy(source, target, load_sem.at[index])
        copy.start()
        return copy

    key_load = load(0, key_in, key)
    value_load = load(1, value_in, value)

    barrier = pltpu.get_barrier_semaphore()

    def greet(i, carry):
        pl.semaphore_signal(
            barrier, inc=1, device_id={"ctx": (me + i) % SEQ_BLOCKS}, device_id_type=pl.DeviceIdType.MESH
        )
        return carry

    lax.fori_loop(1, SEQ_BLOCKS, greet, 0)
    for other in (sibling, across):
        pl.semaphore_signal(barrier, inc=1, device_id={"tp": other}, device_id_type=pl.DeviceIdType.MESH)

    key_load.wait()
    value_load.wait()

    def gate(s):
        gated[s] = (key[s].astype(jnp.float32) * value[s].astype(jnp.float32)).astype(jnp.bfloat16)

    for_blocks(gate)
    cot_load = load(2, cot_in, cot.at[part])
    first_load = load(3, first_in, first_wide)
    turn_load = load(4, turn_in, turn)
    second_load = load(5, second_in, second_wide)
    taps_load = load(6, taps_in, taps)
    last_load = load(7, last_in, last_wide)
    weight_load = load(8, weight_in, weight)
    query_load = load(9, query_in, query)
    pl.semaphore_wait(barrier, SEQ_BLOCKS + 1)

    def to_device(source, target, send_sem, recv_sem, device):
        return pltpu.make_async_remote_copy(
            src_ref=source,
            dst_ref=target,
            send_sem=send_sem,
            recv_sem=recv_sem,
            device_id=device,
            device_id_type=pl.DeviceIdType.MESH,
        )

    def exchange(source, target, sems):
        def step(i, carry):
            peer = (me + i) % SEQ_BLOCKS
            to_device(source.at[peer], target.at[me], sems.at[0], sems.at[1], {"ctx": peer}).start()
            return carry

        lax.fori_loop(1, SEQ_BLOCKS, step, 0)
        target[me] = source[me]

    def whole_exchange(source, target, sems):
        blocks = pl.ds(0, SEQ_BLOCKS - 1)
        return to_device(source.at[blocks], target.at[blocks], sems.at[0], sems.at[1], {"tp": across})

    def arrived(source, target, sems):
        whole_exchange(source, target, sems).wait_recv()

    def sent(source, target, sems):
        whole_exchange(source, target, sems).wait_send()

    exchange(gated, gated_got, gated_sems)

    near = pltpu.make_async_remote_copy(
        src_ref=cot_in,
        dst_ref=cot.at[part],
        send_sem=near_sems.at[0],
        recv_sem=near_sems.at[1],
        device_id={"tp": sibling},
        device_id_type=pl.DeviceIdType.MESH,
    )
    near.start()

    def cot_block(p, parity, half, q):
        columns = pl.ds(q * 256 + parity * LANES, LANES)
        return cot.at[p, pl.ds(half * 256, 256), columns]

    def chunk_bytes(p, parity, half, sems, device):
        window = cot.at[p, pl.ds(half * 256, 256), pl.ds(0, 512)]
        return to_device(window, window, sems.at[0, parity, half], sems.at[1, parity, half], device)

    def far_start(parity, half):
        for q in range(4):
            columns = pl.ds(q * 256 + parity * LANES, LANES)
            to_device(
                cot_in.at[pl.ds(half * 256, 256), columns], cot_block(part, parity, half, q),
                far_sems.at[0, parity, half], far_sems.at[1, parity, half], {"tp": across},
            ).start()

    def relay_start(parity, half):
        chunk_bytes(across, parity, half, far_sems, {"tp": across}).wait_recv()
        for q in range(4):
            block = cot_block(across, parity, half, q)
            to_device(
                block, block, relay_sems.at[0, parity, half], relay_sems.at[1, parity, half], {"tp": sibling}
            ).start()

    def relay_arrived(parity, half):
        chunk_bytes(diagonal, parity, half, relay_sems, {"tp": sibling}).wait_recv()

    taps_load.wait()
    first_load.wait()
    turn_load.wait()
    second_load.wait()
    first[...] = first_wide[...].astype(jnp.bfloat16)
    second[...] = second_wide[...].astype(jnp.bfloat16)
    taps_to_grid(taps, skip_ref, grid)
    spectrum_of(grid, first, turn, second, mixed, taps_spec, True)

    def mix_features(p, fresh, halves=(0, 1)):
        columns = pl.ds(pl.multiple_of(p * 1024, 1024), 1024)
        for half in halves:
            rows = pl.ds(half * 256, 256)
            term = lax.dot_general(
                weight[:, columns], cot[p, rows, :], (((1,), (1,)), ((), ())),
                preferred_element_type=jnp.float32,
            )
            if fresh:
                grad_mixed[:, rows] = term
            else:
                grad_mixed[:, rows] += term

    def mix_chunk(p, parity, half):
        rows = pl.ds(half * 256, 256)
        left = [
            weight[:, pl.ds(pl.multiple_of(p * 1024 + q * 256 + parity * LANES, LANES), LANES)] for q in range(4)
        ]
        right = [cot[p, rows, pl.ds(q * 256 + parity * LANES, LANES)] for q in range(4)]
        grad_mixed[:, rows] += lax.dot_general(
            jnp.concatenate(left, axis=1), jnp.concatenate(right, axis=1), (((1,), (1,)), ((), ())),
            preferred_element_type=jnp.float32,
        )

    cot_load.wait()
    weight_load.wait()
    mix_features(part, True)
    last_load.wait()
    last[...] = last_wide[...].astype(jnp.bfloat16)
    query_load.wait()

    arrived(gated, gated_got, gated_sems)
    far_start(0, 0)
    take_blocks(gated_got, grid)
    spectrum_of(grid, first, turn, second, mixed, gated_spec, False)
    product_to(mixed, taps_spec, gated_spec, False)
    signal_of(mixed, last, turn, second, spec, grid)
    give_blocks(grid, conv)
    exchange(conv, conv_got, conv_sems)

    def half_exchange(half, source, target, peer):
        columns = pl.ds(half * 256, 256)
        return to_device(
            source.at[peer, :, columns], target.at[me, :, columns], grad_sems.at[0, half], grad_sems.at[1, half],
            {"ctx": peer},
        )

    def whole_half(half):
        blocks, columns = pl.ds(0, SEQ_BLOCKS - 1), pl.ds(half * 256, 256)
        return to_device(
            grad.at[blocks, :, columns], grad_got.at[blocks, :, columns], grad_sems.at[0, half],
            grad_sems.at[1, half], {"tp": across},
        )

    def take_chunk(parity, half):
        relay_start(parity, half)
        mix_chunk(across, parity, half)
        relay_arrived(parity, half)
        mix_chunk(diagonal, parity, half)

    def send_gradient(half):
        columns = pl.ds(half * 256, 256)

        def cotangent(s):
            grad[s, :, columns] = (
                grad_mixed[block_rows(s), columns] * query[s, :, columns].astype(jnp.float32)
            ).astype(jnp.bfloat16)

        for_blocks(cotangent)

        def step(i, carry):
            half_exchange(half, grad, grad_got, (me + i) % SEQ_BLOCKS).start()
            return carry

        lax.fori_loop(1, SEQ_BLOCKS, step, 0)
        grad_got[me, :, columns] = grad[me, :, columns]

    near.wait_recv()
    mix_features(sibling, False)
    arrived(conv, conv_got, conv_sems)
    far_start(0, 1)
    far_start(1, 0)
    far_start(1, 1)

    def gate_output(s):
        gate_mixed[block_rows(s), :] = (
            query[s].astype(jnp.float32) * conv_got[s].astype(jnp.float32)
        ).astype(jnp.bfloat16)

    for_blocks(gate_output)

    z, y, x = me // 8, me // 2 % 4, me % 2
    chip = part // 2

    def peer_of(order, stage, k):
        if order == stage:
            return (z + k) % 4, {"ctx": (z + k) % 4 * 8 + y * 2 + x}, z
        return (y + k) % 4, {"ctx": z * 8 + (y + k) % 4 * 2 + x}, y

    def first_columns(order, piece):
        if order == 0:
            return pl.ds(0, 1024) if piece == 0 else pl.ds((piece - 1) * 512, 512)
        if piece == 0:
            return pl.ds(pl.multiple_of(chip * 512, 512), 512)
        return pl.ds(pl.multiple_of((1 - chip) * 512 + (piece - 1) * 256, 256), 256)

    def first_send(order, piece, k):
        place, device, own = peer_of(order, 0, k)
        columns = first_columns(order, piece)
        return to_device(
            terms[order].at[place, :, columns], terms_got[order].at[own, :, columns],
            terms_sems.at[0, order, piece, k - 1], terms_sems.at[1, order, piece, k - 1], device,
        )

    def first_arrival(order, piece, k):
        place, device, own = peer_of(order, 0, 4 - k)
        columns = first_columns(order, piece)
        return to_device(
            terms[order].at[place, :, columns], terms_got[order].at[place, :, columns],
            terms_sems.at[0, order, piece, k - 1], terms_sems.at[1, order, piece, k - 1], device,
        )

    def second_send(order, parity, k):
        place, device, own = peer_of(order, 1, k)
        columns = pl.ds(parity * LANES, LANES)
        return to_device(
            second_terms[order].at[place, :, columns], second_got[order].at[own, :, columns],
            second_sems.at[0, order, parity, k - 1], second_sems.at[1, order, parity, k - 1], device,
        )

    def second_arrival(order, parity, k):
        place, device, own = peer_of(order, 1, 4 - k)
        columns = pl.ds(parity * LANES, LANES)
        return to_device(
            second_terms[order].at[place, :, columns], second_got[order].at[place, :, columns],
            second_sems.at[0, order, parity, k - 1], second_sems.at[1, order, parity, k - 1], device,
        )

    def side_of(order):
        return to_device(
            third[order], third_got[order], third_sems.at[0, order], third_sems.at[1, order],
            {"ctx": me + 1 - 2 * x},
        )

    def keep_term(p, q, parity, term):
        columns = pl.ds(pl.multiple_of(parity * 512 + q * LANES, LANES), LANES)
        terms[0][p, :, columns] = term[:Z_FIRST]
        columns = pl.ds(pl.multiple_of(p // 2 * 512 + parity * 256 + p % 2 * LANES, LANES), LANES)
        terms[1][q, :, columns] = term[Z_FIRST:]

    def make_terms():
        def step(i, carry):
            p, q = chip * 2 + i // 4, i % 4
            columns = pl.ds(pl.multiple_of(q * 256, 256), 256)
            term = dot(gate_mixed[...], cot[p, :, columns]).astype(jnp.bfloat16)
            for parity in range(2):
                keep_term(p, q, parity, term[:, parity * LANES : (parity + 1) * LANES])
            return carry

        lax.fori_loop(0, 8, step, 0)

    def make_late_terms(parity):
        def step(i, carry):
            p, q = (1 - chip) * 2 + i // 2, i % 2 * 2
            right = [
                cot[p, :, pl.ds(pl.multiple_of((q + n) * 256 + parity * LANES, LANES), LANES)] for n in range(2)
            ]
            term = dot(gate_mixed[...], jnp.concatenate(right, axis=1)).astype(jnp.bfloat16)
            for n in range(2):
                keep_term(p, q + n, parity, term[:, n * LANES : (n + 1) * LANES])
            return carry

        lax.fori_loop(0, 4, step, 0)

    def on_chip(place, piece):
        here = place // 2 == chip
        return here if piece == 0 else jnp.logical_not(here)

    def send_terms(piece):
        for k in (2, 1, 3):
            first_send(1, piece, k).start()

            @pl.when(on_chip((z + k) % 4, piece))
            def _():
                first_send(0, piece, k).start()

    make_terms()
    send_terms(0)
    take_chunk(0, 0)
    take_chunk(0, 1)
    make_late_terms(0)
    send_terms(1)
    take_chunk(1, 0)
    send_gradient(0)
    take_chunk(1, 1)
    send_gradient(1)
    make_late_terms(1)
    send_terms(2)

    def query_gradient(s):
        query_res[s] = (grad_mixed[block_rows(s), :] * conv_got[s].astype(jnp.float32)).astype(jnp.bfloat16)

    for_blocks(query_gradient)

    def summed(order, stage, held, got, columns):
        own = z if order == stage else y
        total = held[order][own, :, columns].astype(jnp.float32)
        for k in (1, 2, 3):
            total += got[order][(own + k) % 4, :, columns].astype(jnp.float32)
        return total

    def first_sum(piece):
        parities = (0, 1) if piece == 0 else (piece - 1,)
        owner = chip if piece == 0 else 1 - chip
        for k in (1, 3, 2):
            first_arrival(1, piece, k).wait_recv()
        for parity in parities:
            for n in range(2):
                start = pl.multiple_of(owner * 512 + parity * 256 + n * LANES, LANES)
                total = summed(1, 0, terms, terms_got, pl.ds(start, LANES))
                second_terms[1][owner * 2 + n, :, pl.ds(parity * LANES, LANES)] = total.astype(jnp.bfloat16)
        for k in (2, 1, 3):

            @pl.when(on_chip((z + k) % 4, piece))
            def _():
                for parity in parities:
                    second_send(1, parity, k).start()

        @pl.when(on_chip(z, piece))
        def _():
            for k in (1, 3, 2):
                first_arrival(0, piece, k).wait_recv()
            for parity in parities:
                for place in range(4):
                    total = summed(0, 0, terms, terms_got, pl.ds(parity * 512 + place * LANES, LANES))
                    second_terms[0][place, :, pl.ds(parity * LANES, LANES)] = total.astype(jnp.bfloat16)
                for k in (2, 1, 3):
                    second_send(0, parity, k).start()

    first_sum(0)

    for half in range(2):
        whole_half(half).wait_recv()
    take_blocks(grad_got, grid)
    spectrum_of(grid, first, turn, second, mixed, grad_spec, False)
    product_to(mixed, taps_spec, grad_spec, True)
    signal_of(mixed, last, turn, second, spec, grid)
    give_blocks(grid, back)
    exchange(back, back_got, back_sems)
    first_sum(1)
    product_to(mixed, gated_spec, grad_spec, True)
    signal_of(mixed, last, turn, second, spec, grid)
    grid_to_taps(grid, taps_res)
    skip_gradient(grad_got, gated_got, skip_out)

    first_sum(2)
    arrived(back, back_got, back_sems)

    def gate_input(s):
        back_f = back_got[s].astype(jnp.float32)
        key_res[s] = (back_f * value[s].astype(jnp.float32)).astype(jnp.bfloat16)
        value_res[s] = (back_f * key[s].astype(jnp.float32)).astype(jnp.bfloat16)

    for_blocks(gate_input)
    for parity in range(2):
        columns = pl.ds(parity * LANES, LANES)
        for order in range(2):
            for k in (1, 3, 2):
                second_arrival(order, parity, k).wait_recv()

        @pl.when(x == parity)
        def _():
            for order, (start, stop) in enumerate(TERM_SPANS):
                weight_res[start:stop, :] = summed(order, 1, second_terms, second_got, columns)

        @pl.when(x != parity)
        def _():
            for order in range(2):
                third[order][...] = summed(order, 1, second_terms, second_got, columns).astype(jnp.bfloat16)
                side_of(order).start()

    for order, (start, stop) in enumerate(TERM_SPANS):
        side_of(order).wait_recv()
        weight_res[start:stop, :] += third_got[order][...].astype(jnp.float32)

    sent(gated, gated_got, gated_sems)
    sent(conv, conv_got, conv_sems)
    for half in range(2):
        whole_half(half).wait_send()
    sent(back, back_got, back_sems)
    for k in (1, 2, 3):
        for piece in range(3):
            first_send(1, piece, k).wait_send()

            @pl.when(on_chip((z + k) % 4, piece))
            def _():
                first_send(0, piece, k).wait_send()

        for order in range(2):
            for parity in range(2):
                second_send(order, parity, k).wait_send()
    for order in range(2):
        side_of(order).wait_send()
    near.wait_send()
    for parity in range(2):
        for half in range(2):
            chunk_bytes(part, parity, half, far_sems, {"tp": across}).wait_send()
            chunk_bytes(across, parity, half, relay_sems, {"tp": sibling}).wait_send()


def hand_over(*refs):
    sources, targets, sems = refs[:6], refs[6:12], refs[12]
    copies = [pltpu.make_async_copy(a, b, sems.at[i]) for i, (a, b) in enumerate(zip(sources, targets))]
    for copy in copies:
        copy.start()
    for copy in copies:
        copy.wait()


def body(query_gate, key_branch, value_branch, filter_taps, skip_gain, out_weight, out_grad):
    constants = [jnp.asarray(t) for t in tables()]
    blocks = (SEQ_BLOCKS, CHANS, 2 * COLS)
    bf16, f32 = jnp.bfloat16, jnp.float32
    in_hbm = pl.BlockSpec(memory_space=pl.ANY)
    in_vmem = pl.BlockSpec(memory_space=pltpu.VMEM)
    block_buffer = pltpu.VMEM(blocks, bf16)
    spec_buffer = pltpu.VMEM((CHANS * ROWS, 2 * COLS), f32)
    spans = [stop - start for start, stop in TERM_SPANS]
    terms_buffers = [pltpu.VMEM((4, rows, 1024), bf16) for rows in spans]
    second_buffers = [pltpu.VMEM((4, rows, 256), bf16) for rows in spans]
    third_buffers = [pltpu.VMEM((rows, LANES), bf16) for rows in spans]
    dma = pltpu.SemaphoreType.DMA
    shapes = (
        jax.ShapeDtypeStruct(blocks, bf16),
        jax.ShapeDtypeStruct(blocks, bf16),
        jax.ShapeDtypeStruct(blocks, bf16),
        jax.ShapeDtypeStruct(filter_taps.shape, f32),
        jax.ShapeDtypeStruct((1, CHANS), f32),
        jax.ShapeDtypeStruct((512, LANES), f32),
    )
    results = pl.pallas_call(
        kernel,
        out_shape=tuple(pltpu.VMEM(t.shape, t.dtype) for t in shapes),
        in_specs=[in_hbm] * 4 + [in_vmem] + [in_hbm] * 6,
        out_specs=[in_vmem] * 6,
        scratch_shapes=[
            block_buffer, block_buffer, block_buffer,
            pltpu.VMEM(filter_taps.shape, f32),
            pltpu.VMEM(out_weight.shape, bf16),
            *[pltpu.VMEM(t.shape, f32) for t in constants],
            *[pltpu.VMEM(t.shape, bf16) for t in (constants[0], constants[1], constants[3])],
            pltpu.VMEM((4, 512, 1024), bf16),
            *[block_buffer] * 8,
            *terms_buffers * 2, *second_buffers * 2, *third_buffers * 2,
            pltpu.VMEM((512, 512), f32),
            pltpu.VMEM((512, 512), bf16),
            pltpu.VMEM((2, CHANS * ROWS, LANES), f32),
            pltpu.VMEM((CHANS * ROWS, 2 * COLS), bf16),
            *[spec_buffer] * 4,
            dma((10,)),
            dma((2,)), dma((2,)), dma((2, 2)), dma((2,)),
            dma((2, 2, 3, 3)), dma((2, 2, 2, 3)), dma((2, 2)),
            dma((2,)), dma((2, 2, 2)), dma((2, 2, 2)),
        ],
        compiler_params=pltpu.CompilerParams(
            collective_id=0, has_side_effects=True, vmem_limit_bytes=56 * 1024 * 1024
        ),
    )(
        query_gate.reshape(blocks), key_branch.reshape(blocks), value_branch.reshape(blocks), filter_taps,
        skip_gain[None, :], out_weight, out_grad, *constants,
    )
    grad_query, grad_key, grad_value, grad_filter, grad_skip, grad_weight = pl.pallas_call(
        hand_over,
        out_shape=shapes,
        in_specs=[in_vmem] * 6,
        out_specs=[in_hbm] * 6,
        scratch_shapes=[dma((6,))],
        compiler_params=pltpu.CompilerParams(vmem_limit_bytes=16 * 1024 * 1024),
    )(*results)
    shape = query_gate.shape
    return (
        grad_query.reshape(shape), grad_key.reshape(shape), grad_value.reshape(shape),
        grad_filter, grad_skip[0], grad_weight,
    )


def solution(mesh):
    placed = (
        P("tp", "ctx"),
        P("tp", "ctx"),
        P("tp", "ctx"),
        P(("tp", "ctx"), None),
        P(("tp", "ctx")),
        P("tp", None),
        P("ctx", "tp"),
    )
    return jax.shard_map(
        body,
        mesh=mesh,
        in_specs=placed,
        out_specs=(
            P("tp", "ctx"),
            P("tp", "ctx"),
            P("tp", "ctx"),
            P(("tp", "ctx"), None),
            P(("tp", "ctx")),
            P("tp", "ctx"),
        ),
        check_vma=False,
    )
```

```python
import numpy as np
import ml_dtypes
import jax
import jax.numpy as jnp
from jax import lax
from jax.experimental import pallas as pl
from jax.experimental.pallas import tpu as pltpu
from jax.sharding import PartitionSpec as P

ROWS = 64
COLS = 256
LANES = 128
CHANS = 16
SEQ_BLOCKS = 32
Z_FIRST = 192
TERM_SPANS = ((0, Z_FIRST), (Z_FIRST, 512))


def bf16_pair(values):
    high = values.astype(ml_dtypes.bfloat16)
    low = (values - high.astype(np.float64)).astype(ml_dtypes.bfloat16)
    return high, low


def tables():
    ka = np.arange(ROWS) + 0.5
    phase_a = 2.0 * np.pi * np.outer(ka, np.arange(ROWS)) / (2 * ROWS)
    first = np.concatenate([np.cos(phase_a), -np.sin(phase_a)], axis=0)
    high, low = bf16_pair(first)
    first = np.concatenate([high, low, high], axis=1)
    last = np.concatenate([np.cos(phase_a).T, np.sin(phase_a).T], axis=1) / (ROWS * COLS)
    last = last.astype(ml_dtypes.bfloat16)
    last = np.concatenate([last, last], axis=1)
    phase_t = 2.0 * np.pi * np.outer(ka, np.arange(COLS)) / (2 * ROWS * COLS)
    turn = np.concatenate([np.cos(phase_t), np.sin(phase_t)], axis=1).astype(np.float32)
    phase_b = 2.0 * np.pi * (np.outer(np.arange(COLS), np.arange(COLS)) % COLS) / COLS
    cos_b, sin_b = np.cos(phase_b), np.sin(phase_b)
    second = np.block([[cos_b, -sin_b], [sin_b, cos_b]]).astype(ml_dtypes.bfloat16)
    return [t.astype(np.float32) for t in (first, last, turn, second)]


def dot(left, right):
    return jnp.dot(left, right, preferred_element_type=jnp.float32)


def turned(re, im, turn_ref):
    cos, sin = turn_ref[:, :COLS], turn_ref[:, COLS:]
    return re * cos + im * sin, im * cos - re * sin


def take_blocks(blocks_ref, grid):
    def step(s, carry):
        block = blocks_ref[s].astype(jnp.float32)
        for part in range(4):
            rows = pl.ds(pl.multiple_of(s * 32 + part // 2 * CHANS, CHANS), CHANS)
            grid[part % 2, rows, :] = block[:, part * LANES : (part + 1) * LANES]
        return carry

    lax.fori_loop(0, SEQ_BLOCKS, step, 0, unroll=4)


def second_stage(mixed, second_ref, out):
    out[...] = dot(mixed[...], second_ref[...])


def spectrum_of(grid, first_ref, turn_ref, second_ref, mixed, out, wide):
    def step(c, carry):
        rows = pl.ds(c, ROWS, stride=CHANS)
        signal = jnp.concatenate([grid[0, rows, :], grid[1, rows, :]], axis=1)
        high = signal.astype(jnp.bfloat16)
        if wide:
            low = (signal - high.astype(jnp.float32)).astype(jnp.bfloat16)
            left, right = first_ref[...], jnp.concatenate([high, high, low], axis=0)
        else:
            left, right = first_ref[:, : 2 * ROWS], jnp.concatenate([high, high], axis=0)
        part = dot(left, right)
        re, im = turned(part[:ROWS], part[ROWS:], turn_ref)
        rows = pl.ds(pl.multiple_of(c * ROWS, ROWS), ROWS)
        mixed[rows, :COLS] = re.astype(jnp.bfloat16)
        mixed[rows, COLS:] = im.astype(jnp.bfloat16)
        return carry

    lax.fori_loop(0, CHANS, step, 0, unroll=16)
    second_stage(mixed, second_ref, out)


def product_to(mixed, left, right, conj):
    def step(i, carry):
        rows = pl.ds(pl.multiple_of(i * ROWS, ROWS), ROWS)
        lr, li = left[rows, :COLS], left[rows, COLS:]
        rr, ri = right[rows, :COLS], right[rows, COLS:]
        if conj:
            re, im = lr * rr + li * ri, li * rr - lr * ri
        else:
            re, im = lr * rr - li * ri, -(lr * ri + li * rr)
        mixed[rows, :COLS] = re.astype(jnp.bfloat16)
        mixed[rows, COLS:] = im.astype(jnp.bfloat16)
        return carry

    lax.fori_loop(0, CHANS, step, 0, unroll=2)


def signal_of(mixed, last_ref, turn_ref, second_ref, spec, grid):
    second_stage(mixed, second_ref, spec)

    def step(c, carry):
        rows = pl.ds(pl.multiple_of(c * ROWS, ROWS), ROWS)
        re, im = turned(spec[rows, :COLS], spec[rows, COLS:], turn_ref)
        both = jnp.concatenate([re, im], axis=0)
        high = both.astype(jnp.bfloat16)
        low = (both - high.astype(jnp.float32)).astype(jnp.bfloat16)
        signal = dot(last_ref[...], jnp.concatenate([high, low], axis=0))
        for half in range(2):
            grid[half, pl.ds(c, ROWS, stride=CHANS), :] = signal[:, half * LANES : (half + 1) * LANES]
        return carry

    lax.fori_loop(0, CHANS, step, 0, unroll=16)


def give_block(grid, blocks_ref, s):
    for part in range(4):
        rows = pl.ds(pl.multiple_of(s * 32 + part // 2 * CHANS, CHANS), CHANS)
        blocks_ref[s, :, part * LANES : (part + 1) * LANES] = grid[part % 2, rows, :].astype(jnp.bfloat16)


def taps_to_grid(taps, skip_ref, grid):
    for a in range(ROWS):
        for half in range(2):
            start = a * COLS + half * LANES
            grid[half, a * CHANS : (a + 1) * CHANS, :] = taps[:, start : start + LANES]
    row = lax.broadcasted_iota(jnp.int32, (CHANS, CHANS), 0)
    col = lax.broadcasted_iota(jnp.int32, (CHANS, CHANS), 1)
    skip = jnp.sum(jnp.where(row == col, skip_ref[...], 0.0), axis=1, keepdims=True)
    lane = lax.broadcasted_iota(jnp.int32, (CHANS, LANES), 1)
    grid[0, :CHANS, :] += jnp.where(lane == 0, skip, 0.0)


def grid_to_taps(grid, taps):
    for a in range(ROWS):
        for half in range(2):
            start = a * COLS + half * LANES
            taps[:, start : start + LANES] = grid[half, a * CHANS : (a + 1) * CHANS, :]


def skip_gradient(grad, gated, out_ref):
    def step(s, total):
        return total + grad[s].astype(jnp.float32) * gated[s].astype(jnp.float32)

    total = lax.fori_loop(0, SEQ_BLOCKS, step, jnp.zeros((CHANS, 2 * COLS), jnp.float32))
    total = jnp.sum(total, axis=1, keepdims=True)
    row = lax.broadcasted_iota(jnp.int32, (CHANS, CHANS), 0)
    col = lax.broadcasted_iota(jnp.int32, (CHANS, CHANS), 1)
    out_ref[...] = jnp.sum(jnp.where(row == col, total, 0.0), axis=0, keepdims=True)


def for_blocks(step, unroll=4):
    def body(s, carry):
        step(s)
        return carry

    lax.fori_loop(0, SEQ_BLOCKS, body, 0, unroll=unroll)


def block_rows(s):
    return pl.ds(pl.multiple_of(s * CHANS, CHANS), CHANS)


def kernel(
    query_in, key_in, value_in, taps_in, skip_ref, weight_in, cot_in, first_in, last_in, turn_in, second_in,
    query_res, key_res, value_res, taps_res, skip_out, weight_res,
    query, key, value, taps, weight, first_wide, last_wide, turn, second_wide, first, last, second,
    cot, gated, gated_got, conv, conv_got, grad, grad_got, back, back_got,
    terms_z, terms_y, terms_got_z, terms_got_y, second_z, second_y, second_got_z, second_got_y,
    third_z, third_y, third_got_z, third_got_y, grad_mixed, gate_mixed,
    grid, mixed, spec, taps_spec, gated_spec, grad_spec,
    load_sem, gated_sems, conv_sems, grad_sems, back_sems, terms_sems, second_sems, third_sems,
    near_sems, far_sems, relay_sems,
):
    terms, terms_got = (terms_z, terms_y), (terms_got_z, terms_got_y)
    second_terms, second_got = (second_z, second_y), (second_got_z, second_got_y)
    third, third_got = (third_z, third_y), (third_got_z, third_got_y)
    me = lax.axis_index("ctx")
    part = lax.axis_index("tp")
    sibling = part + 1 - 2 * (part % 2)
    across = (part + 2) % 4
    diagonal = (sibling + 2) % 4

    def load(index, source, target):
        copy = pltpu.make_async_copy(source, target, load_sem.at[index])
        copy.start()
        return copy

    key_load = load(0, key_in, key)
    value_load = load(1, value_in, value)

    barrier = pltpu.get_barrier_semaphore()

    def greet(i, carry):
        pl.semaphore_signal(
            barrier, inc=1, device_id={"ctx": (me + i) % SEQ_BLOCKS}, device_id_type=pl.DeviceIdType.MESH
        )
        return carry

    lax.fori_loop(1, SEQ_BLOCKS, greet, 0)
    for other in (sibling, across):
        pl.semaphore_signal(barrier, inc=1, device_id={"tp": other}, device_id_type=pl.DeviceIdType.MESH)

    key_load.wait()
    value_load.wait()

    def gate(s):
        gated[s] = (key[s].astype(jnp.float32) * value[s].astype(jnp.float32)).astype(jnp.bfloat16)

    for_blocks(gate)
    cot_load = load(2, cot_in, cot.at[part])
    first_load = load(3, first_in, first_wide)
    turn_load = load(4, turn_in, turn)
    second_load = load(5, second_in, second_wide)
    taps_load = load(6, taps_in, taps)
    last_load = load(7, last_in, last_wide)
    weight_load = load(8, weight_in, weight)
    query_load = load(9, query_in, query)
    pl.semaphore_wait(barrier, SEQ_BLOCKS + 1)

    def to_device(source, target, send_sem, recv_sem, device):
        return pltpu.make_async_remote_copy(
            src_ref=source,
            dst_ref=target,
            send_sem=send_sem,
            recv_sem=recv_sem,
            device_id=device,
            device_id_type=pl.DeviceIdType.MESH,
        )

    def exchange(source, target, sems):
        def step(i, carry):
            peer = (me + i) % SEQ_BLOCKS
            to_device(source.at[peer], target.at[me], sems.at[0], sems.at[1], {"ctx": peer}).start()
            return carry

        lax.fori_loop(1, SEQ_BLOCKS, step, 0)
        target[me] = source[me]

    def give_and_exchange(target_blocks, got, sems):
        def step(i, carry):
            peer = (me + i) % SEQ_BLOCKS
            give_block(grid, target_blocks, peer)

            @pl.when(i < SEQ_BLOCKS)
            def _():
                to_device(target_blocks.at[peer], got.at[me], sems.at[0], sems.at[1], {"ctx": peer}).start()

            return carry

        lax.fori_loop(1, SEQ_BLOCKS + 1, step, 0, unroll=4)
        got[me] = target_blocks[me]

    def whole_exchange(source, target, sems):
        blocks = pl.ds(0, SEQ_BLOCKS - 1)
        return to_device(source.at[blocks], target.at[blocks], sems.at[0], sems.at[1], {"tp": across})

    def arrived(source, target, sems):
        whole_exchange(source, target, sems).wait_recv()

    def sent(source, target, sems):
        whole_exchange(source, target, sems).wait_send()

    exchange(gated, gated_got, gated_sems)

    near = pltpu.make_async_remote_copy(
        src_ref=cot_in,
        dst_ref=cot.at[part],
        send_sem=near_sems.at[0],
        recv_sem=near_sems.at[1],
        device_id={"tp": sibling},
        device_id_type=pl.DeviceIdType.MESH,
    )
    near.start()

    def cot_block(p, parity, half, q):
        columns = pl.ds(q * 256 + parity * LANES, LANES)
        return cot.at[p, pl.ds(half * 256, 256), columns]

    def chunk_bytes(p, parity, half, sems, device):
        window = cot.at[p, pl.ds(half * 256, 256), pl.ds(0, 512)]
        return to_device(window, window, sems.at[0, parity, half], sems.at[1, parity, half], device)

    def far_start(parity, half):
        for q in range(4):
            columns = pl.ds(q * 256 + parity * LANES, LANES)
            to_device(
                cot_in.at[pl.ds(half * 256, 256), columns], cot_block(part, parity, half, q),
                far_sems.at[0, parity, half], far_sems.at[1, parity, half], {"tp": across},
            ).start()

    def relay_start(parity, half):
        chunk_bytes(across, parity, half, far_sems, {"tp": across}).wait_recv()
        for q in range(4):
            block = cot_block(across, parity, half, q)
            to_device(
                block, block, relay_sems.at[0, parity, half], relay_sems.at[1, parity, half], {"tp": sibling}
            ).start()

    def relay_arrived(parity, half):
        chunk_bytes(diagonal, parity, half, relay_sems, {"tp": sibling}).wait_recv()

    taps_load.wait()
    first_load.wait()
    turn_load.wait()
    second_load.wait()
    first[...] = first_wide[...].astype(jnp.bfloat16)
    second[...] = second_wide[...].astype(jnp.bfloat16)
    taps_to_grid(taps, skip_ref, grid)
    spectrum_of(grid, first, turn, second, mixed, taps_spec, True)

    def mix_features(p, fresh, halves=(0, 1)):
        columns = pl.ds(pl.multiple_of(p * 1024, 1024), 1024)
        for half in halves:
            rows = pl.ds(half * 256, 256)
            term = lax.dot_general(
                weight[:, columns], cot[p, rows, :], (((1,), (1,)), ((), ())),
                preferred_element_type=jnp.float32,
            )
            if fresh:
                grad_mixed[:, rows] = term
            else:
                grad_mixed[:, rows] += term

    def mix_chunk(p, parity, half):
        rows = pl.ds(half * 256, 256)
        left = [
            weight[:, pl.ds(pl.multiple_of(p * 1024 + q * 256 + parity * LANES, LANES), LANES)] for q in range(4)
        ]
        right = [cot[p, rows, pl.ds(q * 256 + parity * LANES, LANES)] for q in range(4)]
        grad_mixed[:, rows] += lax.dot_general(
            jnp.concatenate(left, axis=1), jnp.concatenate(right, axis=1), (((1,), (1,)), ((), ())),
            preferred_element_type=jnp.float32,
        )

    cot_load.wait()
    weight_load.wait()
    mix_features(part, True)
    last_load.wait()
    last[...] = last_wide[...].astype(jnp.bfloat16)
    query_load.wait()

    arrived(gated, gated_got, gated_sems)
    far_start(0, 0)
    take_blocks(gated_got, grid)
    spectrum_of(grid, first, turn, second, mixed, gated_spec, False)
    product_to(mixed, taps_spec, gated_spec, False)
    signal_of(mixed, last, turn, second, spec, grid)
    give_and_exchange(conv, conv_got, conv_sems)
    far_start(0, 1)

    def half_exchange(half, source, target, peer):
        columns = pl.ds(half * 256, 256)
        return to_device(
            source.at[peer, :, columns], target.at[me, :, columns], grad_sems.at[0, half], grad_sems.at[1, half],
            {"ctx": peer},
        )

    def whole_half(half):
        blocks, columns = pl.ds(0, SEQ_BLOCKS - 1), pl.ds(half * 256, 256)
        return to_device(
            grad.at[blocks, :, columns], grad_got.at[blocks, :, columns], grad_sems.at[0, half],
            grad_sems.at[1, half], {"tp": across},
        )

    def take_chunk(parity, half):
        relay_start(parity, half)
        mix_chunk(across, parity, half)
        relay_arrived(parity, half)
        mix_chunk(diagonal, parity, half)

    def send_gradient(half):
        columns = pl.ds(half * 256, 256)

        def cotangent(s):
            grad[s, :, columns] = (
                grad_mixed[block_rows(s), columns] * query[s, :, columns].astype(jnp.float32)
            ).astype(jnp.bfloat16)

        for_blocks(cotangent)

        def step(i, carry):
            half_exchange(half, grad, grad_got, (me + i) % SEQ_BLOCKS).start()
            return carry

        lax.fori_loop(1, SEQ_BLOCKS, step, 0)
        grad_got[me, :, columns] = grad[me, :, columns]

    near.wait_recv()
    mix_features(sibling, False)
    arrived(conv, conv_got, conv_sems)
    far_start(1, 0)
    far_start(1, 1)

    def gate_output(s):
        gate_mixed[block_rows(s), :] = (
            query[s].astype(jnp.float32) * conv_got[s].astype(jnp.float32)
        ).astype(jnp.bfloat16)

    for_blocks(gate_output)

    z, y, x = me // 8, me // 2 % 4, me % 2
    chip = part // 2

    def peer_of(order, stage, k):
        if order == stage:
            return (z + k) % 4, {"ctx": (z + k) % 4 * 8 + y * 2 + x}, z
        return (y + k) % 4, {"ctx": z * 8 + (y + k) % 4 * 2 + x}, y

    def first_columns(order, piece):
        if order == 0:
            return pl.ds(0, 1024) if piece == 0 else pl.ds((piece - 1) * 512, 512)
        if piece == 0:
            return pl.ds(pl.multiple_of(chip * 512, 512), 512)
        return pl.ds(pl.multiple_of((1 - chip) * 512 + (piece - 1) * 256, 256), 256)

    def first_send(order, piece, k):
        place, device, own = peer_of(order, 0, k)
        columns = first_columns(order, piece)
        return to_device(
            terms[order].at[place, :, columns], terms_got[order].at[own, :, columns],
            terms_sems.at[0, order, piece, k - 1], terms_sems.at[1, order, piece, k - 1], device,
        )

    def first_arrival(order, piece, k):
        place, device, own = peer_of(order, 0, 4 - k)
        columns = first_columns(order, piece)
        return to_device(
            terms[order].at[place, :, columns], terms_got[order].at[place, :, columns],
            terms_sems.at[0, order, piece, k - 1], terms_sems.at[1, order, piece, k - 1], device,
        )

    def second_send(order, parity, k):
        place, device, own = peer_of(order, 1, k)
        columns = pl.ds(parity * LANES, LANES)
        return to_device(
            second_terms[order].at[place, :, columns], second_got[order].at[own, :, columns],
            second_sems.at[0, order, parity, k - 1], second_sems.at[1, order, parity, k - 1], device,
        )

    def second_arrival(order, parity, k):
        place, device, own = peer_of(order, 1, 4 - k)
        columns = pl.ds(parity * LANES, LANES)
        return to_device(
            second_terms[order].at[place, :, columns], second_got[order].at[place, :, columns],
            second_sems.at[0, order, parity, k - 1], second_sems.at[1, order, parity, k - 1], device,
        )

    def side_of(order):
        return to_device(
            third[order], third_got[order], third_sems.at[0, order], third_sems.at[1, order],
            {"ctx": me + 1 - 2 * x},
        )

    def keep_term(p, q, parity, term):
        columns = pl.ds(pl.multiple_of(parity * 512 + q * LANES, LANES), LANES)
        terms[0][p, :, columns] = term[:Z_FIRST]
        columns = pl.ds(pl.multiple_of(p // 2 * 512 + parity * 256 + p % 2 * LANES, LANES), LANES)
        terms[1][q, :, columns] = term[Z_FIRST:]

    def make_terms():
        def step(i, carry):
            p, q = chip * 2 + i // 4, i % 4
            columns = pl.ds(pl.multiple_of(q * 256, 256), 256)
            term = dot(gate_mixed[...], cot[p, :, columns]).astype(jnp.bfloat16)
            for parity in range(2):
                keep_term(p, q, parity, term[:, parity * LANES : (parity + 1) * LANES])
            return carry

        lax.fori_loop(0, 8, step, 0)

    def make_late_terms(parity):
        def step(i, carry):
            p, q = (1 - chip) * 2 + i // 2, i % 2 * 2
            right = [
                cot[p, :, pl.ds(pl.multiple_of((q + n) * 256 + parity * LANES, LANES), LANES)] for n in range(2)
            ]
            term = dot(gate_mixed[...], jnp.concatenate(right, axis=1)).astype(jnp.bfloat16)
            for n in range(2):
                keep_term(p, q + n, parity, term[:, n * LANES : (n + 1) * LANES])
            return carry

        lax.fori_loop(0, 4, step, 0)

    def on_chip(place, piece):
        here = place // 2 == chip
        return here if piece == 0 else jnp.logical_not(here)

    def send_terms(piece):
        for k in (2, 1, 3):
            first_send(1, piece, k).start()

            @pl.when(on_chip((z + k) % 4, piece))
            def _():
                first_send(0, piece, k).start()

    make_terms()
    send_terms(0)
    take_chunk(0, 0)
    take_chunk(0, 1)
    make_late_terms(0)
    send_terms(1)
    take_chunk(1, 0)
    send_gradient(0)
    take_chunk(1, 1)
    send_gradient(1)
    make_late_terms(1)
    send_terms(2)

    def query_gradient(s):
        query_res[s] = (grad_mixed[block_rows(s), :] * conv_got[s].astype(jnp.float32)).astype(jnp.bfloat16)

    for_blocks(query_gradient)

    def summed(order, stage, held, got, columns):
        own = z if order == stage else y
        total = held[order][own, :, columns].astype(jnp.float32)
        for k in (1, 2, 3):
            total += got[order][(own + k) % 4, :, columns].astype(jnp.float32)
        return total

    def first_sum(piece):
        parities = (0, 1) if piece == 0 else (piece - 1,)
        owner = chip if piece == 0 else 1 - chip
        for k in (1, 3, 2):
            first_arrival(1, piece, k).wait_recv()
        for parity in parities:
            for n in range(2):
                start = pl.multiple_of(owner * 512 + parity * 256 + n * LANES, LANES)
                total = summed(1, 0, terms, terms_got, pl.ds(start, LANES))
                second_terms[1][owner * 2 + n, :, pl.ds(parity * LANES, LANES)] = total.astype(jnp.bfloat16)
        for k in (2, 1, 3):

            @pl.when(on_chip((z + k) % 4, piece))
            def _():
                for parity in parities:
                    second_send(1, parity, k).start()

        @pl.when(on_chip(z, piece))
        def _():
            for k in (1, 3, 2):
                first_arrival(0, piece, k).wait_recv()
            for parity in parities:
                for place in range(4):
                    total = summed(0, 0, terms, terms_got, pl.ds(parity * 512 + place * LANES, LANES))
                    second_terms[0][place, :, pl.ds(parity * LANES, LANES)] = total.astype(jnp.bfloat16)
                for k in (2, 1, 3):
                    second_send(0, parity, k).start()

    first_sum(0)

    for half in range(2):
        whole_half(half).wait_recv()
    take_blocks(grad_got, grid)
    spectrum_of(grid, first, turn, second, mixed, grad_spec, False)
    product_to(mixed, taps_spec, grad_spec, True)
    signal_of(mixed, last, turn, second, spec, grid)
    give_and_exchange(back, back_got, back_sems)
    first_sum(1)
    product_to(mixed, gated_spec, grad_spec, True)
    signal_of(mixed, last, turn, second, spec, grid)
    grid_to_taps(grid, taps_res)
    skip_gradient(grad_got, gated_got, skip_out)

    first_sum(2)
    arrived(back, back_got, back_sems)

    def gate_input(s):
        back_f = back_got[s].astype(jnp.float32)
        key_res[s] = (back_f * value[s].astype(jnp.float32)).astype(jnp.bfloat16)
        value_res[s] = (back_f * key[s].astype(jnp.float32)).astype(jnp.bfloat16)

    for_blocks(gate_input)
    for parity in range(2):
        columns = pl.ds(parity * LANES, LANES)
        for order in range(2):
            for k in (1, 3, 2):
                second_arrival(order, parity, k).wait_recv()

        @pl.when(x == parity)
        def _():
            for order, (start, stop) in enumerate(TERM_SPANS):
                weight_res[start:stop, :] = summed(order, 1, second_terms, second_got, columns)

        @pl.when(x != parity)
        def _():
            for order in range(2):
                third[order][...] = summed(order, 1, second_terms, second_got, columns).astype(jnp.bfloat16)
                side_of(order).start()

    for order, (start, stop) in enumerate(TERM_SPANS):
        side_of(order).wait_recv()
        weight_res[start:stop, :] += third_got[order][...].astype(jnp.float32)

    sent(gated, gated_got, gated_sems)
    sent(conv, conv_got, conv_sems)
    for half in range(2):
        whole_half(half).wait_send()
    sent(back, back_got, back_sems)
    for k in (1, 2, 3):
        for piece in range(3):
            first_send(1, piece, k).wait_send()

            @pl.when(on_chip((z + k) % 4, piece))
            def _():
                first_send(0, piece, k).wait_send()

        for order in range(2):
            for parity in range(2):
                second_send(order, parity, k).wait_send()
    for order in range(2):
        side_of(order).wait_send()
    near.wait_send()
    for parity in range(2):
        for half in range(2):
            chunk_bytes(part, parity, half, far_sems, {"tp": across}).wait_send()
            chunk_bytes(across, parity, half, relay_sems, {"tp": sibling}).wait_send()


def hand_over(*refs):
    sources, targets, sems = refs[:6], refs[6:12], refs[12]
    copies = [pltpu.make_async_copy(a, b, sems.at[i]) for i, (a, b) in enumerate(zip(sources, targets))]
    for copy in copies:
        copy.start()
    for copy in copies:
        copy.wait()


def body(query_gate, key_branch, value_branch, filter_taps, skip_gain, out_weight, out_grad):
    constants = [jnp.asarray(t) for t in tables()]
    blocks = (SEQ_BLOCKS, CHANS, 2 * COLS)
    bf16, f32 = jnp.bfloat16, jnp.float32
    in_hbm = pl.BlockSpec(memory_space=pl.ANY)
    in_vmem = pl.BlockSpec(memory_space=pltpu.VMEM)
    block_buffer = pltpu.VMEM(blocks, bf16)
    spec_buffer = pltpu.VMEM((CHANS * ROWS, 2 * COLS), f32)
    spans = [stop - start for start, stop in TERM_SPANS]
    terms_buffers = [pltpu.VMEM((4, rows, 1024), bf16) for rows in spans]
    second_buffers = [pltpu.VMEM((4, rows, 256), bf16) for rows in spans]
    third_buffers = [pltpu.VMEM((rows, LANES), bf16) for rows in spans]
    dma = pltpu.SemaphoreType.DMA
    shapes = (
        jax.ShapeDtypeStruct(blocks, bf16),
        jax.ShapeDtypeStruct(blocks, bf16),
        jax.ShapeDtypeStruct(blocks, bf16),
        jax.ShapeDtypeStruct(filter_taps.shape, f32),
        jax.ShapeDtypeStruct((1, CHANS), f32),
        jax.ShapeDtypeStruct((512, LANES), f32),
    )
    results = pl.pallas_call(
        kernel,
        out_shape=tuple(pltpu.VMEM(t.shape, t.dtype) for t in shapes),
        in_specs=[in_hbm] * 4 + [in_vmem] + [in_hbm] * 6,
        out_specs=[in_vmem] * 6,
        scratch_shapes=[
            block_buffer, block_buffer, block_buffer,
            pltpu.VMEM(filter_taps.shape, f32),
            pltpu.VMEM(out_weight.shape, bf16),
            *[pltpu.VMEM(t.shape, f32) for t in constants],
            *[pltpu.VMEM(t.shape, bf16) for t in (constants[0], constants[1], constants[3])],
            pltpu.VMEM((4, 512, 1024), bf16),
            *[block_buffer] * 8,
            *terms_buffers * 2, *second_buffers * 2, *third_buffers * 2,
            pltpu.VMEM((512, 512), f32),
            pltpu.VMEM((512, 512), bf16),
            pltpu.VMEM((2, CHANS * ROWS, LANES), f32),
            pltpu.VMEM((CHANS * ROWS, 2 * COLS), bf16),
            *[spec_buffer] * 4,
            dma((10,)),
            dma((2,)), dma((2,)), dma((2, 2)), dma((2,)),
            dma((2, 2, 3, 3)), dma((2, 2, 2, 3)), dma((2, 2)),
            dma((2,)), dma((2, 2, 2)), dma((2, 2, 2)),
        ],
        compiler_params=pltpu.CompilerParams(
            collective_id=0, has_side_effects=True, vmem_limit_bytes=56 * 1024 * 1024
        ),
    )(
        query_gate.reshape(blocks), key_branch.reshape(blocks), value_branch.reshape(blocks), filter_taps,
        skip_gain[None, :], out_weight, out_grad, *constants,
    )
    grad_query, grad_key, grad_value, grad_filter, grad_skip, grad_weight = pl.pallas_call(
        hand_over,
        out_shape=shapes,
        in_specs=[in_vmem] * 6,
        out_specs=[in_hbm] * 6,
        scratch_shapes=[dma((6,))],
        compiler_params=pltpu.CompilerParams(vmem_limit_bytes=16 * 1024 * 1024),
    )(*results)
    shape = query_gate.shape
    return (
        grad_query.reshape(shape), grad_key.reshape(shape), grad_value.reshape(shape),
        grad_filter, grad_skip[0], grad_weight,
    )


def solution(mesh):
    placed = (
        P("tp", "ctx"),
        P("tp", "ctx"),
        P("tp", "ctx"),
        P(("tp", "ctx"), None),
        P(("tp", "ctx")),
        P("tp", None),
        P("ctx", "tp"),
    )
    return jax.shard_map(
        body,
        mesh=mesh,
        in_specs=placed,
        out_specs=(
            P("tp", "ctx"),
            P("tp", "ctx"),
            P("tp", "ctx"),
            P(("tp", "ctx"), None),
            P(("tp", "ctx")),
            P("tp", "ctx"),
        ),
        check_vma=False,
    )
```

```python
import numpy as np
import ml_dtypes
import jax
import jax.numpy as jnp
from jax import lax
from jax.experimental import pallas as pl
from jax.experimental.pallas import tpu as pltpu
from jax.sharding import PartitionSpec as P

ROWS = 64
COLS = 256
LANES = 128
CHANS = 16
SEQ_BLOCKS = 32
Z_FIRST = 208
TERM_SPANS = ((0, Z_FIRST), (Z_FIRST, 512))


def bf16_pair(values):
    high = values.astype(ml_dtypes.bfloat16)
    low = (values - high.astype(np.float64)).astype(ml_dtypes.bfloat16)
    return high, low


def tables():
    ka = np.arange(ROWS) + 0.5
    phase_a = 2.0 * np.pi * np.outer(ka, np.arange(ROWS)) / (2 * ROWS)
    first = np.concatenate([np.cos(phase_a), -np.sin(phase_a)], axis=0)
    high, low = bf16_pair(first)
    first = np.concatenate([high, low, high], axis=1)
    last = np.concatenate([np.cos(phase_a).T, np.sin(phase_a).T], axis=1) / (ROWS * COLS)
    last = last.astype(ml_dtypes.bfloat16)
    last = np.concatenate([last, last], axis=1)
    phase_t = 2.0 * np.pi * np.outer(ka, np.arange(COLS)) / (2 * ROWS * COLS)
    turn = np.concatenate([np.cos(phase_t), np.sin(phase_t)], axis=1).astype(np.float32)
    phase_b = 2.0 * np.pi * (np.outer(np.arange(COLS), np.arange(COLS)) % COLS) / COLS
    cos_b, sin_b = np.cos(phase_b), np.sin(phase_b)
    second = np.block([[cos_b, -sin_b], [sin_b, cos_b]]).astype(ml_dtypes.bfloat16)
    return [t.astype(np.float32) for t in (first, last, turn, second)]


def dot(left, right):
    return jnp.dot(left, right, preferred_element_type=jnp.float32)


def turned(re, im, turn_ref):
    cos, sin = turn_ref[:, :COLS], turn_ref[:, COLS:]
    return re * cos + im * sin, im * cos - re * sin


def take_blocks(blocks_ref, grid):
    def step(s, carry):
        block = blocks_ref[s].astype(jnp.float32)
        for part in range(4):
            rows = pl.ds(pl.multiple_of(s * 32 + part // 2 * CHANS, CHANS), CHANS)
            grid[part % 2, rows, :] = block[:, part * LANES : (part + 1) * LANES]
        return carry

    lax.fori_loop(0, SEQ_BLOCKS, step, 0, unroll=4)


def second_stage(mixed, second_ref, out):
    out[...] = dot(mixed[...], second_ref[...])


def spectrum_of(grid, first_ref, turn_ref, second_ref, mixed, out, wide):
    def step(c, carry):
        rows = pl.ds(c, ROWS, stride=CHANS)
        signal = jnp.concatenate([grid[0, rows, :], grid[1, rows, :]], axis=1)
        high = signal.astype(jnp.bfloat16)
        if wide:
            low = (signal - high.astype(jnp.float32)).astype(jnp.bfloat16)
            left, right = first_ref[...], jnp.concatenate([high, high, low], axis=0)
        else:
            left, right = first_ref[:, : 2 * ROWS], jnp.concatenate([high, high], axis=0)
        part = dot(left, right)
        re, im = turned(part[:ROWS], part[ROWS:], turn_ref)
        rows = pl.ds(pl.multiple_of(c * ROWS, ROWS), ROWS)
        mixed[rows, :COLS] = re.astype(jnp.bfloat16)
        mixed[rows, COLS:] = im.astype(jnp.bfloat16)
        return carry

    lax.fori_loop(0, CHANS, step, 0, unroll=16)
    second_stage(mixed, second_ref, out)


def product_to(mixed, left, right, conj):
    def step(i, carry):
        rows = pl.ds(pl.multiple_of(i * ROWS, ROWS), ROWS)
        lr, li = left[rows, :COLS], left[rows, COLS:]
        rr, ri = right[rows, :COLS], right[rows, COLS:]
        if conj:
            re, im = lr * rr + li * ri, li * rr - lr * ri
        else:
            re, im = lr * rr - li * ri, -(lr * ri + li * rr)
        mixed[rows, :COLS] = re.astype(jnp.bfloat16)
        mixed[rows, COLS:] = im.astype(jnp.bfloat16)
        return carry

    lax.fori_loop(0, CHANS, step, 0, unroll=2)


def signal_of(mixed, last_ref, turn_ref, second_ref, spec, grid):
    second_stage(mixed, second_ref, spec)

    def step(c, carry):
        rows = pl.ds(pl.multiple_of(c * ROWS, ROWS), ROWS)
        re, im = turned(spec[rows, :COLS], spec[rows, COLS:], turn_ref)
        both = jnp.concatenate([re, im], axis=0)
        high = both.astype(jnp.bfloat16)
        low = (both - high.astype(jnp.float32)).astype(jnp.bfloat16)
        signal = dot(last_ref[...], jnp.concatenate([high, low], axis=0))
        for half in range(2):
            grid[half, pl.ds(c, ROWS, stride=CHANS), :] = signal[:, half * LANES : (half + 1) * LANES]
        return carry

    lax.fori_loop(0, CHANS, step, 0, unroll=16)


def give_block(grid, blocks_ref, s):
    for part in range(4):
        rows = pl.ds(pl.multiple_of(s * 32 + part // 2 * CHANS, CHANS), CHANS)
        blocks_ref[s, :, part * LANES : (part + 1) * LANES] = grid[part % 2, rows, :].astype(jnp.bfloat16)


def taps_to_grid(taps, skip_ref, grid):
    for a in range(ROWS):
        for half in range(2):
            start = a * COLS + half * LANES
            grid[half, a * CHANS : (a + 1) * CHANS, :] = taps[:, start : start + LANES]
    row = lax.broadcasted_iota(jnp.int32, (CHANS, CHANS), 0)
    col = lax.broadcasted_iota(jnp.int32, (CHANS, CHANS), 1)
    skip = jnp.sum(jnp.where(row == col, skip_ref[...], 0.0), axis=1, keepdims=True)
    lane = lax.broadcasted_iota(jnp.int32, (CHANS, LANES), 1)
    grid[0, :CHANS, :] += jnp.where(lane == 0, skip, 0.0)


def grid_to_taps(grid, taps):
    for a in range(ROWS):
        for half in range(2):
            start = a * COLS + half * LANES
            taps[:, start : start + LANES] = grid[half, a * CHANS : (a + 1) * CHANS, :]


def skip_gradient(grad, gated, out_ref):
    def step(s, total):
        return total + grad[s].astype(jnp.float32) * gated[s].astype(jnp.float32)

    total = lax.fori_loop(0, SEQ_BLOCKS, step, jnp.zeros((CHANS, 2 * COLS), jnp.float32))
    total = jnp.sum(total, axis=1, keepdims=True)
    row = lax.broadcasted_iota(jnp.int32, (CHANS, CHANS), 0)
    col = lax.broadcasted_iota(jnp.int32, (CHANS, CHANS), 1)
    out_ref[...] = jnp.sum(jnp.where(row == col, total, 0.0), axis=0, keepdims=True)


def for_blocks(step, unroll=4):
    def body(s, carry):
        step(s)
        return carry

    lax.fori_loop(0, SEQ_BLOCKS, body, 0, unroll=unroll)


def block_rows(s):
    return pl.ds(pl.multiple_of(s * CHANS, CHANS), CHANS)


def kernel(
    query_in, key_in, value_in, taps_in, skip_ref, weight_in, cot_in, first_in, last_in, turn_in, second_in,
    query_res, key_res, value_res, taps_res, skip_out, weight_res,
    query, key, value, taps, weight, first_wide, last_wide, turn, second_wide, first, last, second,
    cot, gated, gated_got, conv, conv_got, grad, grad_got, back, back_got,
    terms_z, terms_y, terms_got_z, terms_got_y, second_z, second_y, second_got_z, second_got_y,
    third_z, third_y, third_got_z, third_got_y, grad_mixed, gate_mixed,
    grid, mixed, spec, taps_spec, gated_spec, grad_spec,
    load_sem, gated_sems, conv_sems, grad_sems, back_sems, terms_sems, second_sems, third_sems,
    near_sems, far_sems, relay_sems,
):
    terms, terms_got = (terms_z, terms_y), (terms_got_z, terms_got_y)
    second_terms, second_got = (second_z, second_y), (second_got_z, second_got_y)
    third, third_got = (third_z, third_y), (third_got_z, third_got_y)
    me = lax.axis_index("ctx")
    part = lax.axis_index("tp")
    sibling = part + 1 - 2 * (part % 2)
    across = (part + 2) % 4
    diagonal = (sibling + 2) % 4

    def load(index, source, target):
        copy = pltpu.make_async_copy(source, target, load_sem.at[index])
        copy.start()
        return copy

    key_load = load(0, key_in, key)
    value_load = load(1, value_in, value)

    barrier = pltpu.get_barrier_semaphore()

    def greet(i, carry):
        pl.semaphore_signal(
            barrier, inc=1, device_id={"ctx": (me + i) % SEQ_BLOCKS}, device_id_type=pl.DeviceIdType.MESH
        )
        return carry

    lax.fori_loop(1, SEQ_BLOCKS, greet, 0)
    for other in (sibling, across):
        pl.semaphore_signal(barrier, inc=1, device_id={"tp": other}, device_id_type=pl.DeviceIdType.MESH)

    key_load.wait()
    value_load.wait()

    def gate(s):
        gated[s] = (key[s].astype(jnp.float32) * value[s].astype(jnp.float32)).astype(jnp.bfloat16)

    for_blocks(gate)
    cot_load = load(2, cot_in, cot.at[part])
    first_load = load(3, first_in, first_wide)
    turn_load = load(4, turn_in, turn)
    second_load = load(5, second_in, second_wide)
    taps_load = load(6, taps_in, taps)
    last_load = load(7, last_in, last_wide)
    weight_load = load(8, weight_in, weight)
    query_load = load(9, query_in, query)
    pl.semaphore_wait(barrier, SEQ_BLOCKS + 1)

    def to_device(source, target, send_sem, recv_sem, device):
        return pltpu.make_async_remote_copy(
            src_ref=source,
            dst_ref=target,
            send_sem=send_sem,
            recv_sem=recv_sem,
            device_id=device,
            device_id_type=pl.DeviceIdType.MESH,
        )

    def exchange(source, target, sems):
        def step(i, carry):
            peer = (me + i) % SEQ_BLOCKS
            to_device(source.at[peer], target.at[me], sems.at[0], sems.at[1], {"ctx": peer}).start()
            return carry

        lax.fori_loop(1, SEQ_BLOCKS, step, 0)
        target[me] = source[me]

    def give_and_exchange(target_blocks, got, sems):
        def step(i, carry):
            peer = (me + i) % SEQ_BLOCKS
            give_block(grid, target_blocks, peer)

            @pl.when(i < SEQ_BLOCKS)
            def _():
                to_device(target_blocks.at[peer], got.at[me], sems.at[0], sems.at[1], {"ctx": peer}).start()

            return carry

        lax.fori_loop(1, SEQ_BLOCKS + 1, step, 0, unroll=4)
        got[me] = target_blocks[me]

    def whole_exchange(source, target, sems):
        blocks = pl.ds(0, SEQ_BLOCKS - 1)
        return to_device(source.at[blocks], target.at[blocks], sems.at[0], sems.at[1], {"tp": across})

    def arrived(source, target, sems):
        whole_exchange(source, target, sems).wait_recv()

    def sent(source, target, sems):
        whole_exchange(source, target, sems).wait_send()

    exchange(gated, gated_got, gated_sems)

    near = pltpu.make_async_remote_copy(
        src_ref=cot_in,
        dst_ref=cot.at[part],
        send_sem=near_sems.at[0],
        recv_sem=near_sems.at[1],
        device_id={"tp": sibling},
        device_id_type=pl.DeviceIdType.MESH,
    )
    near.start()

    def cot_block(p, parity, half, q):
        columns = pl.ds(q * 256 + parity * LANES, LANES)
        return cot.at[p, pl.ds(half * 256, 256), columns]

    def chunk_bytes(p, parity, half, sems, device):
        window = cot.at[p, pl.ds(half * 256, 256), pl.ds(0, 512)]
        return to_device(window, window, sems.at[0, parity, half], sems.at[1, parity, half], device)

    def far_start(parity, half):
        for q in range(4):
            columns = pl.ds(q * 256 + parity * LANES, LANES)
            to_device(
                cot_in.at[pl.ds(half * 256, 256), columns], cot_block(part, parity, half, q),
                far_sems.at[0, parity, half], far_sems.at[1, parity, half], {"tp": across},
            ).start()

    def relay_start(parity, half):
        chunk_bytes(across, parity, half, far_sems, {"tp": across}).wait_recv()
        for q in range(4):
            block = cot_block(across, parity, half, q)
            to_device(
                block, block, relay_sems.at[0, parity, half], relay_sems.at[1, parity, half], {"tp": sibling}
            ).start()

    def relay_arrived(parity, half):
        chunk_bytes(diagonal, parity, half, relay_sems, {"tp": sibling}).wait_recv()

    taps_load.wait()
    first_load.wait()
    turn_load.wait()
    second_load.wait()
    first[...] = first_wide[...].astype(jnp.bfloat16)
    second[...] = second_wide[...].astype(jnp.bfloat16)
    taps_to_grid(taps, skip_ref, grid)
    spectrum_of(grid, first, turn, second, mixed, taps_spec, True)

    def mix_features(p, fresh, halves=(0, 1)):
        columns = pl.ds(pl.multiple_of(p * 1024, 1024), 1024)
        for half in halves:
            rows = pl.ds(half * 256, 256)
            term = lax.dot_general(
                weight[:, columns], cot[p, rows, :], (((1,), (1,)), ((), ())),
                preferred_element_type=jnp.float32,
            )
            if fresh:
                grad_mixed[:, rows] = term
            else:
                grad_mixed[:, rows] += term

    def mix_chunk(p, parity, half):
        rows = pl.ds(half * 256, 256)
        left = [
            weight[:, pl.ds(pl.multiple_of(p * 1024 + q * 256 + parity * LANES, LANES), LANES)] for q in range(4)
        ]
        right = [cot[p, rows, pl.ds(q * 256 + parity * LANES, LANES)] for q in range(4)]
        grad_mixed[:, rows] += lax.dot_general(
            jnp.concatenate(left, axis=1), jnp.concatenate(right, axis=1), (((1,), (1,)), ((), ())),
            preferred_element_type=jnp.float32,
        )

    cot_load.wait()
    weight_load.wait()
    mix_features(part, True)
    last_load.wait()
    last[...] = last_wide[...].astype(jnp.bfloat16)
    query_load.wait()

    arrived(gated, gated_got, gated_sems)
    far_start(0, 0)
    take_blocks(gated_got, grid)
    spectrum_of(grid, first, turn, second, mixed, gated_spec, False)
    product_to(mixed, taps_spec, gated_spec, False)
    signal_of(mixed, last, turn, second, spec, grid)
    give_and_exchange(conv, conv_got, conv_sems)
    far_start(0, 1)

    def half_exchange(half, source, target, peer):
        columns = pl.ds(half * 256, 256)
        return to_device(
            source.at[peer, :, columns], target.at[me, :, columns], grad_sems.at[0, half], grad_sems.at[1, half],
            {"ctx": peer},
        )

    def whole_half(half):
        blocks, columns = pl.ds(0, SEQ_BLOCKS - 1), pl.ds(half * 256, 256)
        return to_device(
            grad.at[blocks, :, columns], grad_got.at[blocks, :, columns], grad_sems.at[0, half],
            grad_sems.at[1, half], {"tp": across},
        )

    def take_chunk(parity, half):
        relay_start(parity, half)
        mix_chunk(across, parity, half)
        relay_arrived(parity, half)
        mix_chunk(diagonal, parity, half)

    def send_gradient(half):
        columns = pl.ds(half * 256, 256)

        def cotangent(s):
            grad[s, :, columns] = (
                grad_mixed[block_rows(s), columns] * query[s, :, columns].astype(jnp.float32)
            ).astype(jnp.bfloat16)

        for_blocks(cotangent)

        def step(i, carry):
            half_exchange(half, grad, grad_got, (me + i) % SEQ_BLOCKS).start()
            return carry

        lax.fori_loop(1, SEQ_BLOCKS, step, 0)
        grad_got[me, :, columns] = grad[me, :, columns]

    near.wait_recv()
    mix_features(sibling, False)
    arrived(conv, conv_got, conv_sems)
    far_start(1, 0)
    far_start(1, 1)

    def gate_output(s):
        gate_mixed[block_rows(s), :] = (
            query[s].astype(jnp.float32) * conv_got[s].astype(jnp.float32)
        ).astype(jnp.bfloat16)

    for_blocks(gate_output)

    z, y, x = me // 8, me // 2 % 4, me % 2
    chip = part // 2

    def peer_of(order, stage, k):
        if order == stage:
            return (z + k) % 4, {"ctx": (z + k) % 4 * 8 + y * 2 + x}, z
        return (y + k) % 4, {"ctx": z * 8 + (y + k) % 4 * 2 + x}, y

    def first_columns(order, piece):
        if order == 0:
            return pl.ds(0, 1024) if piece == 0 else pl.ds((piece - 1) * 512, 512)
        if piece == 0:
            return pl.ds(pl.multiple_of(chip * 512, 512), 512)
        return pl.ds(pl.multiple_of((1 - chip) * 512 + (piece - 1) * 256, 256), 256)

    def first_send(order, piece, k):
        place, device, own = peer_of(order, 0, k)
        columns = first_columns(order, piece)
        return to_device(
            terms[order].at[place, :, columns], terms_got[order].at[own, :, columns],
            terms_sems.at[0, order, piece, k - 1], terms_sems.at[1, order, piece, k - 1], device,
        )

    def first_arrival(order, piece, k):
        place, device, own = peer_of(order, 0, 4 - k)
        columns = first_columns(order, piece)
        return to_device(
            terms[order].at[place, :, columns], terms_got[order].at[place, :, columns],
            terms_sems.at[0, order, piece, k - 1], terms_sems.at[1, order, piece, k - 1], device,
        )

    def second_send(order, parity, k):
        place, device, own = peer_of(order, 1, k)
        columns = pl.ds(parity * LANES, LANES)
        return to_device(
            second_terms[order].at[place, :, columns], second_got[order].at[own, :, columns],
            second_sems.at[0, order, parity, k - 1], second_sems.at[1, order, parity, k - 1], device,
        )

    def second_arrival(order, parity, k):
        place, device, own = peer_of(order, 1, 4 - k)
        columns = pl.ds(parity * LANES, LANES)
        return to_device(
            second_terms[order].at[place, :, columns], second_got[order].at[place, :, columns],
            second_sems.at[0, order, parity, k - 1], second_sems.at[1, order, parity, k - 1], device,
        )

    def side_of(order):
        return to_device(
            third[order], third_got[order], third_sems.at[0, order], third_sems.at[1, order],
            {"ctx": me + 1 - 2 * x},
        )

    def keep_term(p, q, parity, term):
        columns = pl.ds(pl.multiple_of(parity * 512 + q * LANES, LANES), LANES)
        terms[0][p, :, columns] = term[:Z_FIRST]
        columns = pl.ds(pl.multiple_of(p // 2 * 512 + parity * 256 + p % 2 * LANES, LANES), LANES)
        terms[1][q, :, columns] = term[Z_FIRST:]

    def make_terms():
        def step(i, carry):
            p, q = chip * 2 + i // 4, i % 4
            columns = pl.ds(pl.multiple_of(q * 256, 256), 256)
            term = dot(gate_mixed[...], cot[p, :, columns]).astype(jnp.bfloat16)
            for parity in range(2):
                keep_term(p, q, parity, term[:, parity * LANES : (parity + 1) * LANES])
            return carry

        lax.fori_loop(0, 8, step, 0)

    def make_late_terms(parity):
        def step(i, carry):
            p, q = (1 - chip) * 2 + i // 2, i % 2 * 2
            right = [
                cot[p, :, pl.ds(pl.multiple_of((q + n) * 256 + parity * LANES, LANES), LANES)] for n in range(2)
            ]
            term = dot(gate_mixed[...], jnp.concatenate(right, axis=1)).astype(jnp.bfloat16)
            for n in range(2):
                keep_term(p, q + n, parity, term[:, n * LANES : (n + 1) * LANES])
            return carry

        lax.fori_loop(0, 4, step, 0)

    def on_chip(place, piece):
        here = place // 2 == chip
        return here if piece == 0 else jnp.logical_not(here)

    def send_terms(piece):
        for k in (2, 1, 3):
            first_send(1, piece, k).start()

            @pl.when(on_chip((z + k) % 4, piece))
            def _():
                first_send(0, piece, k).start()

    make_terms()
    send_terms(0)
    take_chunk(0, 0)
    take_chunk(0, 1)
    make_late_terms(0)
    send_terms(1)
    take_chunk(1, 0)
    send_gradient(0)
    take_chunk(1, 1)
    send_gradient(1)
    make_late_terms(1)
    send_terms(2)

    def query_gradient(s):
        query_res[s] = (grad_mixed[block_rows(s), :] * conv_got[s].astype(jnp.float32)).astype(jnp.bfloat16)

    for_blocks(query_gradient)

    def summed(order, stage, held, got, columns):
        own = z if order == stage else y
        total = held[order][own, :, columns].astype(jnp.float32)
        for k in (1, 2, 3):
            total += got[order][(own + k) % 4, :, columns].astype(jnp.float32)
        return total

    def first_sum(piece):
        parities = (0, 1) if piece == 0 else (piece - 1,)
        owner = chip if piece == 0 else 1 - chip
        for k in (1, 3, 2):
            first_arrival(1, piece, k).wait_recv()
        for parity in parities:
            for n in range(2):
                start = pl.multiple_of(owner * 512 + parity * 256 + n * LANES, LANES)
                total = summed(1, 0, terms, terms_got, pl.ds(start, LANES))
                second_terms[1][owner * 2 + n, :, pl.ds(parity * LANES, LANES)] = total.astype(jnp.bfloat16)
        for k in (2, 1, 3):

            @pl.when(on_chip((z + k) % 4, piece))
            def _():
                for parity in parities:
                    second_send(1, parity, k).start()

        @pl.when(on_chip(z, piece))
        def _():
            for k in (1, 3, 2):
                first_arrival(0, piece, k).wait_recv()
            for parity in parities:
                for place in range(4):
                    total = summed(0, 0, terms, terms_got, pl.ds(parity * 512 + place * LANES, LANES))
                    second_terms[0][place, :, pl.ds(parity * LANES, LANES)] = total.astype(jnp.bfloat16)
                for k in (2, 1, 3):
                    second_send(0, parity, k).start()

    first_sum(0)

    for half in range(2):
        whole_half(half).wait_recv()
    take_blocks(grad_got, grid)
    spectrum_of(grid, first, turn, second, mixed, grad_spec, False)
    product_to(mixed, taps_spec, grad_spec, True)
    signal_of(mixed, last, turn, second, spec, grid)
    give_and_exchange(back, back_got, back_sems)
    first_sum(1)
    product_to(mixed, gated_spec, grad_spec, True)
    signal_of(mixed, last, turn, second, spec, grid)
    grid_to_taps(grid, taps_res)
    skip_gradient(grad_got, gated_got, skip_out)

    first_sum(2)
    arrived(back, back_got, back_sems)

    def gate_input(s):
        back_f = back_got[s].astype(jnp.float32)
        key_res[s] = (back_f * value[s].astype(jnp.float32)).astype(jnp.bfloat16)
        value_res[s] = (back_f * key[s].astype(jnp.float32)).astype(jnp.bfloat16)

    for_blocks(gate_input)
    for parity in range(2):
        columns = pl.ds(parity * LANES, LANES)
        for order in range(2):
            for k in (1, 3, 2):
                second_arrival(order, parity, k).wait_recv()

        @pl.when(x == parity)
        def _():
            for order, (start, stop) in enumerate(TERM_SPANS):
                weight_res[start:stop, :] = summed(order, 1, second_terms, second_got, columns)

        @pl.when(x != parity)
        def _():
            for order in range(2):
                third[order][...] = summed(order, 1, second_terms, second_got, columns).astype(jnp.bfloat16)
                side_of(order).start()

    for order, (start, stop) in enumerate(TERM_SPANS):
        side_of(order).wait_recv()
        weight_res[start:stop, :] += third_got[order][...].astype(jnp.float32)

    sent(gated, gated_got, gated_sems)
    sent(conv, conv_got, conv_sems)
    for half in range(2):
        whole_half(half).wait_send()
    sent(back, back_got, back_sems)
    for k in (1, 2, 3):
        for piece in range(3):
            first_send(1, piece, k).wait_send()

            @pl.when(on_chip((z + k) % 4, piece))
            def _():
                first_send(0, piece, k).wait_send()

        for order in range(2):
            for parity in range(2):
                second_send(order, parity, k).wait_send()
    for order in range(2):
        side_of(order).wait_send()
    near.wait_send()
    for parity in range(2):
        for half in range(2):
            chunk_bytes(part, parity, half, far_sems, {"tp": across}).wait_send()
            chunk_bytes(across, parity, half, relay_sems, {"tp": sibling}).wait_send()


def hand_over(*refs):
    sources, targets, sems = refs[:6], refs[6:12], refs[12]
    copies = [pltpu.make_async_copy(a, b, sems.at[i]) for i, (a, b) in enumerate(zip(sources, targets))]
    for copy in copies:
        copy.start()
    for copy in copies:
        copy.wait()


def body(query_gate, key_branch, value_branch, filter_taps, skip_gain, out_weight, out_grad):
    constants = [jnp.asarray(t) for t in tables()]
    blocks = (SEQ_BLOCKS, CHANS, 2 * COLS)
    bf16, f32 = jnp.bfloat16, jnp.float32
    in_hbm = pl.BlockSpec(memory_space=pl.ANY)
    in_vmem = pl.BlockSpec(memory_space=pltpu.VMEM)
    block_buffer = pltpu.VMEM(blocks, bf16)
    spec_buffer = pltpu.VMEM((CHANS * ROWS, 2 * COLS), f32)
    spans = [stop - start for start, stop in TERM_SPANS]
    terms_buffers = [pltpu.VMEM((4, rows, 1024), bf16) for rows in spans]
    second_buffers = [pltpu.VMEM((4, rows, 256), bf16) for rows in spans]
    third_buffers = [pltpu.VMEM((rows, LANES), bf16) for rows in spans]
    dma = pltpu.SemaphoreType.DMA
    shapes = (
        jax.ShapeDtypeStruct(blocks, bf16),
        jax.ShapeDtypeStruct(blocks, bf16),
        jax.ShapeDtypeStruct(blocks, bf16),
        jax.ShapeDtypeStruct(filter_taps.shape, f32),
        jax.ShapeDtypeStruct((1, CHANS), f32),
        jax.ShapeDtypeStruct((512, LANES), f32),
    )
    results = pl.pallas_call(
        kernel,
        out_shape=tuple(pltpu.VMEM(t.shape, t.dtype) for t in shapes),
        in_specs=[in_hbm] * 4 + [in_vmem] + [in_hbm] * 6,
        out_specs=[in_vmem] * 6,
        scratch_shapes=[
            block_buffer, block_buffer, block_buffer,
            pltpu.VMEM(filter_taps.shape, f32),
            pltpu.VMEM(out_weight.shape, bf16),
            *[pltpu.VMEM(t.shape, f32) for t in constants],
            *[pltpu.VMEM(t.shape, bf16) for t in (constants[0], constants[1], constants[3])],
            pltpu.VMEM((4, 512, 1024), bf16),
            *[block_buffer] * 8,
            *terms_buffers * 2, *second_buffers * 2, *third_buffers * 2,
            pltpu.VMEM((512, 512), f32),
            pltpu.VMEM((512, 512), bf16),
            pltpu.VMEM((2, CHANS * ROWS, LANES), f32),
            pltpu.VMEM((CHANS * ROWS, 2 * COLS), bf16),
            *[spec_buffer] * 4,
            dma((10,)),
            dma((2,)), dma((2,)), dma((2, 2)), dma((2,)),
            dma((2, 2, 3, 3)), dma((2, 2, 2, 3)), dma((2, 2)),
            dma((2,)), dma((2, 2, 2)), dma((2, 2, 2)),
        ],
        compiler_params=pltpu.CompilerParams(
            collective_id=0, has_side_effects=True, vmem_limit_bytes=56 * 1024 * 1024
        ),
    )(
        query_gate.reshape(blocks), key_branch.reshape(blocks), value_branch.reshape(blocks), filter_taps,
        skip_gain[None, :], out_weight, out_grad, *constants,
    )
    grad_query, grad_key, grad_value, grad_filter, grad_skip, grad_weight = pl.pallas_call(
        hand_over,
        out_shape=shapes,
        in_specs=[in_vmem] * 6,
        out_specs=[in_hbm] * 6,
        scratch_shapes=[dma((6,))],
        compiler_params=pltpu.CompilerParams(vmem_limit_bytes=16 * 1024 * 1024),
    )(*results)
    shape = query_gate.shape
    return (
        grad_query.reshape(shape), grad_key.reshape(shape), grad_value.reshape(shape),
        grad_filter, grad_skip[0], grad_weight,
    )


def solution(mesh):
    placed = (
        P("tp", "ctx"),
        P("tp", "ctx"),
        P("tp", "ctx"),
        P(("tp", "ctx"), None),
        P(("tp", "ctx")),
        P("tp", None),
        P("ctx", "tp"),
    )
    return jax.shard_map(
        body,
        mesh=mesh,
        in_specs=placed,
        out_specs=(
            P("tp", "ctx"),
            P("tp", "ctx"),
            P("tp", "ctx"),
            P(("tp", "ctx"), None),
            P(("tp", "ctx")),
            P("tp", "ctx"),
        ),
        check_vma=False,
    )
```
